32 devices in a mesh: energy: 16 (over z, y, x), slab: 2 (over core).
Axes of the slice: x: 2, y: 2, z: 4, core: 2. Of those that a mesh axis runs over, the one named last changes fastest.
Arguments:
- green_block: bfloat16 [16, 2, 2, 192, 192], P('energy', 'slab'), may hold values from -0.4375 to 0.4375
- coupling: bfloat16 [16, 2, 2, 192, 192], P('energy', 'slab'), may hold values from -0.4375 to 0.4375
- sigma_lesser: bfloat16 [16, 2, 2, 192, 192], P('energy', 'slab'), may hold values from -6 to 6
- screened: bfloat16 [2, 2, 32, 36864], P('slab', None, None, 'energy'), may hold values from -9 to 9
Outputs:
- sigma_next: bfloat16 [16, 2, 2, 192, 192], P('energy', 'slab')
The draws below stay inside these ranges and needn't reach their ends.
All inputs are finite; a program needn't handle non-finite values.
Results may differ from the reference program's by a relative error of at most 0.0049.
Values may be sent and summed in bfloat16 or wider, within the bound.
A program may use at most 128 MiB of HBM per device.

```python
import math
import jax
import jax.numpy as jnp
from jax import lax

M = 192
BLOCKS = 2
ENERGIES = 16
FREQ = 32
PAIRS = 36864


def block_scale(rng, dims, pieces, least, largest):
    gain, own = 1.0, jax.random.fold_in(rng, 6)
    for dim, blocks in pieces:
        draws = jnp.exp(jax.random.uniform(jax.random.fold_in(own, dim), (blocks,), jnp.float32, least / len(pieces), largest / len(pieces)))
        gain = gain * jnp.repeat(draws, dims[dim] // blocks).reshape([-1 if axis == dim else 1 for axis in range(len(dims))])
    return gain


def noise(rng, dims, scale, reach, split=(), kind=jnp.bfloat16):
    drawn = jax.random.normal(rng, dims, jnp.float32) * scale
    if len(split) > 0:
        drawn = block_scale(rng, dims, split, -0.22, 0.18) * drawn
    return jnp.clip(drawn, min=-reach, max=reach).astype(kind)


def setup_inputs(seed: int = 0) -> dict:
    key_list = jax.random.split(jax.random.key(seed), 5)
    green_block = noise(key_list[0], (ENERGIES, BLOCKS, 2, M, M), M ** -0.5, 0.4375, ((0, 16), (1, 2)))
    coupling = noise(key_list[1], (ENERGIES, BLOCKS, 2, M, M), M ** -0.5, 0.4375, ((0, 16), (1, 2)))
    sigma_lesser = noise(key_list[2], (ENERGIES, BLOCKS, 2, M, M), 1.0, 6.0, ((0, 16), (1, 2)))
    screened = noise(key_list[3], (BLOCKS, 2, FREQ, PAIRS), 1.5, 9.0, ((0, 2), (3, 16)))
    return {"green_block": green_block, "coupling": coupling, "sigma_lesser": sigma_lesser, "screened": screened}


def sandwich(outer, inner):
    outer_real = outer[:, 0].astype(jnp.float32)
    outer_imag = outer[:, 1].astype(jnp.float32)
    inner_real = inner[:, 0].astype(jnp.float32)
    inner_imag = inner[:, 1].astype(jnp.float32)
    forward = "eij,ejk->eik"
    adjoint = "eik,ejk->eij"
    half_real = jnp.einsum(forward, outer_real, inner_real) - jnp.einsum(forward, outer_imag, inner_imag)
    half_imag = jnp.einsum(forward, outer_real, inner_imag) + jnp.einsum(forward, outer_imag, inner_real)
    half_real = lax.optimization_barrier(half_real.astype(jnp.bfloat16)).astype(jnp.float32)
    half_imag = lax.optimization_barrier(half_imag.astype(jnp.bfloat16)).astype(jnp.float32)
    full_real = jnp.einsum(adjoint, half_real, outer_real) + jnp.einsum(adjoint, half_imag, outer_imag)
    full_imag = jnp.einsum(adjoint, half_imag, outer_real) - jnp.einsum(adjoint, half_real, outer_imag)
    return full_real, full_imag


def tables(count):
    length = 2 * count
    rows = jnp.arange(length, dtype=jnp.int32)
    cols = jnp.arange(count, dtype=jnp.int32)
    phases = (rows[:, None] * cols[None, :]) % length
    angles = phases.astype(jnp.float32) * (2.0 * math.pi / length)
    return jnp.cos(angles), jnp.sin(angles)


def reference(green_block, coupling, sigma_lesser, screened):
    high = lax.Precision.HIGHEST
    cosine, sine = tables(ENERGIES)
    results = []
    for position in range(BLOCKS):
        half_own_real, half_own_imag = sandwich(green_block[:, position], sigma_lesser[:, position])
        lesser_real, lesser_imag = half_own_real, half_own_imag
        if position + 1 < BLOCKS:
            half_next_real, half_next_imag = sandwich(coupling[:, position], sigma_lesser[:, position + 1])
            lesser_real = lesser_real + half_next_real
            lesser_imag = lesser_imag + half_next_imag
        flat_real = lesser_real.reshape(ENERGIES, PAIRS)
        flat_imag = lesser_imag.reshape(ENERGIES, PAIRS)
        spec_real = jnp.dot(cosine, flat_real, precision=high) + jnp.dot(sine, flat_imag, precision=high)
        spec_imag = jnp.dot(cosine, flat_imag, precision=high) - jnp.dot(sine, flat_real, precision=high)
        screen_real = screened[position, 0].astype(jnp.float32)
        screen_imag = screened[position, 1].astype(jnp.float32)
        conv_real = spec_real * screen_real - spec_imag * screen_imag
        conv_imag = spec_real * screen_imag + spec_imag * screen_real
        back_real = jnp.dot(cosine.T, conv_real, precision=high) - jnp.dot(sine.T, conv_imag, precision=high)
        back_imag = jnp.dot(cosine.T, conv_imag, precision=high) + jnp.dot(sine.T, conv_real, precision=high)
        joined = jnp.stack([back_real, back_imag], axis=1) / FREQ
        results.append(joined.reshape(ENERGIES, 2, M, M).astype(jnp.bfloat16))
    return jnp.stack(results, axis=1)
```

```python
import functools

import jax
import jax.numpy as jnp
import ml_dtypes
import numpy as np
from jax import lax
from jax.experimental import pallas as pl
from jax.experimental.pallas import tpu as pltpu
from jax.sharding import PartitionSpec as P

MESH = pl.DeviceIdType.MESH
LANES = 128
PITCH = 16


def split(table):
    high = table.astype(ml_dtypes.bfloat16)
    low = (table - high.astype(np.float64)).astype(ml_dtypes.bfloat16)
    return high, low


def make_tables(count, rows, pitch):
    length = 2 * count
    phases = np.outer(np.arange(length), np.arange(count)) % length
    angles = phases * (2.0 * np.pi / length)
    forward, backward = [], []
    same = np.zeros((rows, pitch))
    same[np.arange(rows), np.arange(rows)] = 1.0
    for table in (np.cos(angles), np.sin(angles)):
        wide = np.einsum("ke,rs->rkes", table, same).reshape(rows * length, count * pitch)
        forward.append(split(wide))
        backward.append(split(wide.T / length))
    tables = []
    for pair in (forward, backward):
        tables.append(np.concatenate([pair[0][0], pair[1][0], pair[0][1], pair[1][1]], axis=0))
    spread = np.zeros((count * pitch, count * rows), ml_dtypes.bfloat16)
    for owner in range(count):
        for row in range(rows):
            spread[owner * pitch + row, owner * rows + row] = 1.0
    return tables[0], tables[1], spread, np.ascontiguousarray(spread.T)


def mul(first, second):
    return jnp.dot(first, second, preferred_element_type=jnp.float32)


def mul_t(first, second):
    return lax.dot_general(first, second, (((1,), (1,)), ((), ())), preferred_element_type=jnp.float32)


def sandwich(spread, outer, inner):
    outer_real, outer_imag = outer[0], outer[1]
    inner_real, inner_imag = inner[0], inner[1]
    wide_real = mul(spread, outer_real).astype(jnp.bfloat16)
    wide_imag = mul(spread, outer_imag).astype(jnp.bfloat16)
    half_real = (mul(wide_real, inner_real) - mul(wide_imag, inner_imag)).astype(jnp.bfloat16)
    half_imag = (mul(wide_real, inner_imag) + mul(wide_imag, inner_real)).astype(jnp.bfloat16)
    minus = -outer_imag
    with_real = jnp.concatenate([outer_real[:LANES], minus[:LANES], outer_real[LANES:], minus[LANES:]], axis=0)
    with_imag = jnp.concatenate([outer_imag[:LANES], outer_real[:LANES], outer_imag[LANES:], outer_real[LANES:]], axis=0)
    return mul_t(half_real, with_real) + mul_t(half_imag, with_imag)


def kernel(
    n, slabs, rows, pitch,
    green, couple, sigma, screened, forward, backward, spread, gather,
    out,
    green_v, couple_v, sigma_v, ahead_v, screened_v, forward_v, backward_v, spread_v, gather_v,
    weights, term, send1, recv1, send2, recv2,
    local_sem, slab_send, slab_recv, send1_sem, recv1_sem, send2_sem, recv2_sem,
):
    me = lax.axis_index("energy")
    block = lax.axis_index("slab")
    orbitals = green_v.shape[1]
    length = screened_v.shape[1]
    freq_rows = rows * length
    flat_rows = n * pitch
    tail = orbitals - LANES

    barrier = pltpu.get_barrier_semaphore()

    def greet(step, _):
        pl.semaphore_signal(barrier, inc=1, device_id=(lax.rem(me + step, n), block), device_id_type=MESH)
        return 0

    @pl.when(block > 0)
    def _():
        pl.semaphore_signal(barrier, inc=1, device_id=(me, block - 1), device_id_type=MESH)

    @pl.when(block < slabs - 1)
    def _():
        pl.semaphore_signal(barrier, inc=1, device_id=(me, block + 1), device_id_type=MESH)

    lax.fori_loop(1, n, greet, 0)

    pairs = (
        (green.at[0, 0], green_v), (sigma.at[0, 0], sigma_v), (spread, spread_v), (couple.at[0, 0], couple_v),
        (screened.at[0], screened_v), (forward, forward_v), (backward, backward_v), (gather, gather_v),
    )
    loads = [pltpu.make_async_copy(src, dst, local_sem.at[i]) for i, (src, dst) in enumerate(pairs)]
    for load in loads:
        load.start()

    pl.semaphore_wait(barrier, n - 1 + (block > 0).astype(jnp.int32) + (block < slabs - 1).astype(jnp.int32))

    def to_block_before():
        return pltpu.make_async_remote_copy(
            src_ref=sigma.at[0, 0], dst_ref=ahead_v, send_sem=slab_send, recv_sem=slab_recv,
            device_id=(me, lax.max(block - 1, 0)), device_id_type=MESH,
        )

    @pl.when(block > 0)
    def _():
        to_block_before().start()

    for load in loads[:3]:
        load.wait()
    own = sandwich(spread_v[...], green_v, sigma_v)
    loads[3].wait()

    @pl.when(block == slabs - 1)
    def _():
        send1[...] = own.astype(jnp.bfloat16)

    @pl.when(block < slabs - 1)
    def _():
        term[...] = own
        to_block_before().wait_recv()
        send1[...] = (term[...] + sandwich(spread_v[...], couple_v, ahead_v)).astype(jnp.bfloat16)

    def exchange(src, dst, send_sem, recv_sem):
        def at(ref, index):
            return ref.at[pl.ds(pl.multiple_of(index * pitch, pitch), pitch)]

        def copy(peer, slot):
            return pltpu.make_async_remote_copy(
                src_ref=at(src, peer), dst_ref=at(dst, slot), send_sem=send_sem.at[peer], recv_sem=recv_sem.at[slot],
                device_id=(peer, block), device_id_type=MESH,
            )

        def start(step, _):
            copy(lax.rem(me + step, n), me).start()
            return 0

        def wait_recv(step, _):
            peer = lax.rem(me + step, n)
            copy(peer, peer).wait_recv()
            return 0

        def wait_send(step, _):
            copy(lax.rem(me + step, n), me).wait_send()
            return 0

        lax.fori_loop(1, n, start, 0)
        mine = pl.ds(pl.multiple_of(me * pitch, pitch), pitch)
        dst[mine, :] = src[mine, :]
        return (lambda: lax.fori_loop(1, n, wait_recv, 0)), (lambda: lax.fori_loop(1, n, wait_send, 0))

    arrive1, leave1 = exchange(send1, recv1, send1_sem, recv1_sem)

    loads[4].wait()
    for row in range(rows):
        at = row * orbitals
        where = pl.ds(row * length, length)
        for part in range(2):
            line = screened_v[part, :, at:at + orbitals].astype(jnp.float32)
            last = line[:, LANES:]
            weights[part, where, :LANES] = line[:, :LANES]
            weights[part, where, LANES:] = jnp.concatenate([last, last], axis=1)
    for load in loads[5:]:
        load.wait()

    arrive1()
    arrived = recv1[...]
    by_high = mul(forward_v[:2 * freq_rows], arrived)
    by_low = mul(forward_v[2 * freq_rows:], arrived)
    both = by_high + by_low
    cosine, sine = both[:freq_rows], both[freq_rows:]
    sign = jnp.where(lax.broadcasted_iota(jnp.int32, (1, LANES), 1) < tail, 1.0, -1.0)

    def turn(value):
        return pltpu.roll(value, tail, 1) * sign

    spec_real = cosine[:, :LANES] + sine[:, LANES:2 * LANES]
    spec_imag = cosine[:, LANES:2 * LANES] - sine[:, :LANES]
    spec_tail = cosine[:, 2 * LANES:] + turn(sine[:, 2 * LANES:])
    weight_real, weight_imag = weights[0], weights[1]
    conv = jnp.concatenate(
        [
            spec_real * weight_real[:, :LANES] - spec_imag * weight_imag[:, :LANES],
            spec_real * weight_imag[:, :LANES] + spec_imag * weight_real[:, :LANES],
            spec_tail * weight_real[:, LANES:] - turn(spec_tail) * weight_imag[:, LANES:],
        ],
        axis=1,
    )
    conv_high = conv.astype(jnp.bfloat16)
    conv_low = (conv - conv_high.astype(jnp.float32)).astype(jnp.bfloat16)
    back = mul(backward_v[:2 * flat_rows], conv_high)
    back = back + mul(backward_v[2 * flat_rows:], conv_high)
    back = back + mul(backward_v[:2 * flat_rows], conv_low)
    cosine, sine = back[:flat_rows], back[flat_rows:]
    send2[:, :LANES] = (cosine[:, :LANES] - sine[:, LANES:2 * LANES]).astype(jnp.bfloat16)
    send2[:, LANES:2 * LANES] = (cosine[:, LANES:2 * LANES] + sine[:, :LANES]).astype(jnp.bfloat16)
    send2[:, 2 * LANES:] = (cosine[:, 2 * LANES:] - turn(sine[:, 2 * LANES:])).astype(jnp.bfloat16)

    arrive2, leave2 = exchange(send2, recv2, send2_sem, recv2_sem)
    leave1()

    @pl.when(block > 0)
    def _():
        to_block_before().wait_send()

    arrive2()
    result = mul(gather_v[...], recv2[...]).astype(jnp.bfloat16)
    out[0, 0, 0, :, :LANES] = result[:, :LANES]
    out[0, 0, 1, :, :LANES] = result[:, LANES:2 * LANES]
    out[0, 0, 0, :, LANES:] = result[:, 2 * LANES:2 * LANES + tail]
    out[0, 0, 1, :, LANES:] = result[:, 2 * LANES + tail:]
    leave2()


def shards(n, slabs, green_block, coupling, sigma_lesser, screened):
    orbitals = green_block.shape[-1]
    length = screened.shape[2]
    rows = screened.shape[3] // orbitals
    pitch = -(-rows // PITCH) * PITCH
    assert green_block.shape[0] == 1 and length == 2 * n and rows * n == orbitals and orbitals == LANES + LANES // 2
    tables = make_tables(n, rows, pitch)
    packed = (n * pitch, 2 * orbitals)
    square = (2, orbitals, orbitals)
    bf16 = jnp.bfloat16
    return pl.pallas_call(
        functools.partial(kernel, n, slabs, rows, pitch),
        out_shape=jax.ShapeDtypeStruct(green_block.shape, bf16),
        in_specs=[pl.BlockSpec(memory_space=pl.ANY)] * 8,
        out_specs=pl.BlockSpec(memory_space=pltpu.VMEM),
        scratch_shapes=[
            pltpu.VMEM(square, bf16),
            pltpu.VMEM(square, bf16),
            pltpu.VMEM(square, bf16),
            pltpu.VMEM(square, bf16),
            pltpu.VMEM(screened.shape[1:], bf16),
            *[pltpu.VMEM(table.shape, bf16) for table in tables],
            pltpu.VMEM((2, rows * length, 2 * LANES), jnp.float32),
            pltpu.VMEM(packed, jnp.float32),
            pltpu.VMEM(packed, bf16),
            pltpu.VMEM(packed, bf16),
            pltpu.VMEM(packed, bf16),
            pltpu.VMEM(packed, bf16),
            pltpu.SemaphoreType.DMA((8,)),
            pltpu.SemaphoreType.DMA,
            pltpu.SemaphoreType.DMA,
            *[pltpu.SemaphoreType.DMA((n,))] * 4,
        ],
        compiler_params=pltpu.CompilerParams(
            collective_id=0, has_side_effects=True, vmem_limit_bytes=56 * 1024 * 1024
        ),
        cost_estimate=pl.CostEstimate(flops=10**9, bytes_accessed=4 * 10**6, transcendentals=0),
        name="self_energy",
    )(green_block, coupling, sigma_lesser, screened, *[jnp.asarray(table) for table in tables])


def solution(mesh):
    placed = (
        P("energy", "slab", None, None, None),
        P("energy", "slab", None, None, None),
        P("energy", "slab", None, None, None),
        P("slab", None, None, "energy"),
    )
    return jax.shard_map(
        functools.partial(shards, mesh.shape["energy"], mesh.shape["slab"]),
        mesh=mesh,
        in_specs=placed,
        out_specs=P("energy", "slab", None, None, None),
        check_vma=False,
    )
```

```python
import functools

import jax
import jax.numpy as jnp
import ml_dtypes
import numpy as np
from jax import lax
from jax.experimental import pallas as pl
from jax.experimental.pallas import tpu as pltpu
from jax.sharding import PartitionSpec as P

MESH = pl.DeviceIdType.MESH
LANES = 128
PITCH = 16


def split(table):
    high = table.astype(ml_dtypes.bfloat16)
    low = (table - high.astype(np.float64)).astype(ml_dtypes.bfloat16)
    return high, low


def make_tables(count, rows, pitch):
    length = 2 * count
    phases = np.outer(np.arange(length), np.arange(count)) % length
    angles = phases * (2.0 * np.pi / length)
    forward, backward = [], []
    same = np.zeros((rows, pitch))
    same[np.arange(rows), np.arange(rows)] = 1.0
    for table in (np.cos(angles), np.sin(angles)):
        wide = np.einsum("ke,rs->rkes", table, same).reshape(rows * length, count * pitch)
        forward.append(split(wide))
        backward.append(split(wide.T / length))
    tables = []
    for pair in (forward, backward):
        tables.append(np.concatenate([pair[0][0], pair[1][0], pair[0][1], pair[1][1]], axis=0))
    spread = np.zeros((count * pitch, count * rows), ml_dtypes.bfloat16)
    for owner in range(count):
        for row in range(rows):
            spread[owner * pitch + row, owner * rows + row] = 1.0
    return tables[0], tables[1], spread, np.ascontiguousarray(spread.T)


def mul(first, second):
    return jnp.dot(first, second, preferred_element_type=jnp.float32)


def mul_t(first, second):
    return lax.dot_general(first, second, (((1,), (1,)), ((), ())), preferred_element_type=jnp.float32)


def sandwich(spread, outer, inner):
    outer_real, outer_imag = outer[0], outer[1]
    inner_real, inner_imag = inner[0], inner[1]
    wide_real = mul(spread, outer_real).astype(jnp.bfloat16)
    wide_imag = mul(spread, outer_imag).astype(jnp.bfloat16)
    half_real = (mul(wide_real, inner_real) - mul(wide_imag, inner_imag)).astype(jnp.bfloat16)
    half_imag = (mul(wide_real, inner_imag) + mul(wide_imag, inner_real)).astype(jnp.bfloat16)
    minus = -outer_imag
    with_real = jnp.concatenate([outer_real[:LANES], minus[:LANES], outer_real[LANES:], minus[LANES:]], axis=0)
    with_imag = jnp.concatenate([outer_imag[:LANES], outer_real[:LANES], outer_imag[LANES:], outer_real[LANES:]], axis=0)
    return mul_t(half_real, with_real) + mul_t(half_imag, with_imag)


def kernel(
    n, slabs, rows, pitch,
    green, couple, sigma, screened, forward, backward, spread,
    recv2,
    green_v, couple_v, sigma_v, ahead_v, screened_v, forward_v, backward_v, spread_v,
    weights, term, send1, recv1, send2,
    local_sem, slab_send, slab_recv, send1_sem, recv1_sem, send2_sem, recv2_sem,
):
    me = lax.axis_index("energy")
    block = lax.axis_index("slab")
    orbitals = green_v.shape[1]
    length = screened_v.shape[1]
    freq_rows = rows * length
    flat_rows = n * pitch
    tail = orbitals - LANES

    barrier = pltpu.get_barrier_semaphore()

    def greet(step, _):
        pl.semaphore_signal(barrier, inc=1, device_id=(lax.rem(me + step, n), block), device_id_type=MESH)
        return 0

    @pl.when(block > 0)
    def _():
        pl.semaphore_signal(barrier, inc=1, device_id=(me, block - 1), device_id_type=MESH)

    @pl.when(block < slabs - 1)
    def _():
        pl.semaphore_signal(barrier, inc=1, device_id=(me, block + 1), device_id_type=MESH)

    lax.fori_loop(1, n, greet, 0)

    pairs = (
        (green.at[0, 0], green_v), (sigma.at[0, 0], sigma_v), (spread, spread_v), (couple.at[0, 0], couple_v),
        (screened.at[0], screened_v), (forward, forward_v), (backward, backward_v),
    )
    loads = [pltpu.make_async_copy(src, dst, local_sem.at[i]) for i, (src, dst) in enumerate(pairs)]
    for load in loads:
        load.start()

    def everyone_is_here():
        pl.semaphore_wait(barrier, n - 1 + (block > 0).astype(jnp.int32) + (block < slabs - 1).astype(jnp.int32))

    def to_block_before():
        return pltpu.make_async_remote_copy(
            src_ref=sigma.at[0, 0], dst_ref=ahead_v, send_sem=slab_send, recv_sem=slab_recv,
            device_id=(me, lax.max(block - 1, 0)), device_id_type=MESH,
        )

    @pl.when(block > 0)
    def _():
        everyone_is_here()
        to_block_before().start()

    for load in loads[:3]:
        load.wait()
    own = sandwich(spread_v[...], green_v, sigma_v)
    loads[3].wait()

    @pl.when(block == 0)
    def _():
        everyone_is_here()

    @pl.when(block == slabs - 1)
    def _():
        send1[...] = own.astype(jnp.bfloat16)

    @pl.when(block < slabs - 1)
    def _():
        term[...] = own
        to_block_before().wait_recv()
        send1[...] = (term[...] + sandwich(spread_v[...], couple_v, ahead_v)).astype(jnp.bfloat16)

    def exchange(src, dst, send_sem, recv_sem):
        def at(ref, index):
            return ref.at[pl.ds(pl.multiple_of(index * pitch, pitch), pitch)]

        def copy(peer, slot):
            return pltpu.make_async_remote_copy(
                src_ref=at(src, peer), dst_ref=at(dst, slot), send_sem=send_sem.at[peer], recv_sem=recv_sem.at[slot],
                device_id=(peer, block), device_id_type=MESH,
            )

        def start(step, _):
            copy(lax.rem(me + step, n), me).start()
            return 0

        def wait_recv(step, _):
            peer = lax.rem(me + n - step, n)
            copy(peer, peer).wait_recv()
            return 0

        def wait_send(step, _):
            copy(lax.rem(me + step, n), me).wait_send()
            return 0

        lax.fori_loop(1, n, start, 0)
        keep = pltpu.make_async_copy(at(src, me), at(dst, me), recv_sem.at[me])
        keep.start()
        keep.wait()
        return (lambda: lax.fori_loop(1, n, wait_recv, 0)), (lambda: lax.fori_loop(1, n, wait_send, 0))

    arrive1, leave1 = exchange(send1, recv1, send1_sem, recv1_sem)

    loads[4].wait()
    for row in range(rows):
        at = row * orbitals
        where = pl.ds(row * length, length)
        for part in range(2):
            line = screened_v[part, :, at:at + orbitals].astype(jnp.float32)
            last = line[:, LANES:]
            weights[part, where, :LANES] = line[:, :LANES]
            weights[part, where, LANES:] = jnp.concatenate([last, last], axis=1)
    for load in loads[5:]:
        load.wait()

    arrive1()
    arrived = recv1[...]
    by_high = mul(forward_v[:2 * freq_rows], arrived)
    by_low = mul(forward_v[2 * freq_rows:], arrived)
    both = by_high + by_low
    cosine, sine = both[:freq_rows], both[freq_rows:]
    sign = jnp.where(lax.broadcasted_iota(jnp.int32, (1, LANES), 1) < tail, 1.0, -1.0)

    def turn(value):
        return pltpu.roll(value, tail, 1) * sign

    spec_real = cosine[:, :LANES] + sine[:, LANES:2 * LANES]
    spec_imag = cosine[:, LANES:2 * LANES] - sine[:, :LANES]
    spec_tail = cosine[:, 2 * LANES:] + turn(sine[:, 2 * LANES:])
    weight_real, weight_imag = weights[0], weights[1]
    conv = jnp.concatenate(
        [
            spec_real * weight_real[:, :LANES] - spec_imag * weight_imag[:, :LANES],
            spec_real * weight_imag[:, :LANES] + spec_imag * weight_real[:, :LANES],
            spec_tail * weight_real[:, LANES:] - turn(spec_tail) * weight_imag[:, LANES:],
        ],
        axis=1,
    )
    conv_high = conv.astype(jnp.bfloat16)
    conv_low = (conv - conv_high.astype(jnp.float32)).astype(jnp.bfloat16)
    back = mul(backward_v[:2 * flat_rows], conv_high)
    back = back + mul(backward_v[2 * flat_rows:], conv_high)
    back = back + mul(backward_v[:2 * flat_rows], conv_low)
    cosine, sine = back[:flat_rows], back[flat_rows:]
    send2[:, :LANES] = (cosine[:, :LANES] - sine[:, LANES:2 * LANES]).astype(jnp.bfloat16)
    send2[:, LANES:2 * LANES] = (cosine[:, LANES:2 * LANES] + sine[:, :LANES]).astype(jnp.bfloat16)
    send2[:, 2 * LANES:] = (cosine[:, 2 * LANES:] - turn(sine[:, 2 * LANES:])).astype(jnp.bfloat16)

    arrive2, leave2 = exchange(send2, recv2, send2_sem, recv2_sem)
    leave1()

    @pl.when(block > 0)
    def _():
        to_block_before().wait_send()

    arrive2()
    leave2()


def unpack(gather, packed, out):
    tail = out.shape[-1] - LANES
    result = mul(gather[...], packed[...]).astype(jnp.bfloat16)
    out[0, 0, 0, :, :LANES] = result[:, :LANES]
    out[0, 0, 1, :, :LANES] = result[:, LANES:2 * LANES]
    out[0, 0, 0, :, LANES:] = result[:, 2 * LANES:2 * LANES + tail]
    out[0, 0, 1, :, LANES:] = result[:, 2 * LANES + tail:]


def shards(n, slabs, green_block, coupling, sigma_lesser, screened):
    orbitals = green_block.shape[-1]
    length = screened.shape[2]
    rows = screened.shape[3] // orbitals
    pitch = -(-rows // PITCH) * PITCH
    assert green_block.shape[0] == 1 and length == 2 * n and rows * n == orbitals and orbitals == LANES + LANES // 2
    *tables, gather = make_tables(n, rows, pitch)
    packed = (n * pitch, 2 * orbitals)
    square = (2, orbitals, orbitals)
    bf16 = jnp.bfloat16
    returned = pl.pallas_call(
        functools.partial(kernel, n, slabs, rows, pitch),
        out_shape=jax.ShapeDtypeStruct(packed, bf16),
        in_specs=[pl.BlockSpec(memory_space=pl.ANY)] * 7,
        out_specs=pl.BlockSpec(memory_space=pl.ANY),
        scratch_shapes=[
            pltpu.VMEM(square, bf16),
            pltpu.VMEM(square, bf16),
            pltpu.VMEM(square, bf16),
            pltpu.VMEM(square, bf16),
            pltpu.VMEM(screened.shape[1:], bf16),
            *[pltpu.VMEM(table.shape, bf16) for table in tables],
            pltpu.VMEM((2, rows * length, 2 * LANES), jnp.float32),
            pltpu.VMEM(packed, jnp.float32),
            pltpu.VMEM(packed, bf16),
            pltpu.VMEM(packed, bf16),
            pltpu.VMEM(packed, bf16),
            pltpu.SemaphoreType.DMA((7,)),
            pltpu.SemaphoreType.DMA,
            pltpu.SemaphoreType.DMA,
            *[pltpu.SemaphoreType.DMA((n,))] * 4,
        ],
        compiler_params=pltpu.CompilerParams(
            collective_id=0, has_side_effects=True, vmem_limit_bytes=56 * 1024 * 1024
        ),
        cost_estimate=pl.CostEstimate(flops=10**9, bytes_accessed=4 * 10**6, transcendentals=0),
        name="self_energy",
    )(green_block, coupling, sigma_lesser, screened, *[jnp.asarray(table) for table in tables])
    return pl.pallas_call(
        unpack,
        out_shape=jax.ShapeDtypeStruct(green_block.shape, bf16),
        in_specs=[pl.BlockSpec(memory_space=pltpu.VMEM)] * 2,
        out_specs=pl.BlockSpec(memory_space=pltpu.VMEM),
        name="unpack",
    )(jnp.asarray(gather), returned)


def solution(mesh):
    placed = (
        P("energy", "slab", None, None, None),
        P("energy", "slab", None, None, None),
        P("energy", "slab", None, None, None),
        P("slab", None, None, "energy"),
    )
    return jax.shard_map(
        functools.partial(shards, mesh.shape["energy"], mesh.shape["slab"]),
        mesh=mesh,
        in_specs=placed,
        out_specs=P("energy", "slab", None, None, None),
        check_vma=False,
    )
```

```python
import functools

import jax
import jax.numpy as jnp
import ml_dtypes
import numpy as np
from jax import lax
from jax.experimental import pallas as pl
from jax.experimental.pallas import tpu as pltpu
from jax.sharding import PartitionSpec as P

MESH = pl.DeviceIdType.MESH
LANES = 128
PITCH = 16


def split(table):
    high = table.astype(ml_dtypes.bfloat16)
    low = (table - high.astype(np.float64)).astype(ml_dtypes.bfloat16)
    return high, low


def make_tables(count, rows, pitch):
    length = 2 * count
    phases = np.outer(np.arange(count), np.arange(length)) % length
    angles = phases * (2.0 * np.pi / length)
    same = np.zeros((pitch, rows))
    same[np.arange(rows), np.arange(rows)] = 1.0
    high, low = [], []
    for table in (np.cos(angles), np.sin(angles)):
        wide = np.einsum("dk,sr->dsrk", table / length, same).reshape(count * pitch, rows * length)
        for part, into in zip(split(wide), (high, low)):
            into.append(part)
    gather = np.zeros((count * rows, count * pitch), ml_dtypes.bfloat16)
    for owner in range(count):
        for row in range(rows):
            gather[owner * rows + row, owner * pitch + row] = 1.0
    return np.concatenate(high + low, axis=0), gather


def mul(first, second):
    return jnp.dot(first, second, preferred_element_type=jnp.float32)


def mul_t(first, second):
    return lax.dot_general(first, second, (((1,), (1,)), ((), ())), preferred_element_type=jnp.float32)


def sandwich(outer, inner):
    orbitals = outer.shape[1]
    stacked = outer[...].reshape(2 * orbitals, orbitals)
    by_real = mul(stacked, inner[0])
    by_imag = mul(stacked, inner[1])
    half_real = by_real[:orbitals] - by_imag[orbitals:]
    half_imag = by_imag[:orbitals] + by_real[orbitals:]
    half = jnp.concatenate([half_real.astype(jnp.bfloat16), half_imag.astype(jnp.bfloat16)], axis=0)
    with_real = mul_t(half, jnp.concatenate([outer[0], outer[0, LANES:]], axis=0))
    with_imag = mul_t(half, jnp.concatenate([outer[1], outer[1, LANES:]], axis=0))
    full_real = with_real[:orbitals] + with_imag[orbitals:]
    full_imag = with_real[orbitals:] - with_imag[:orbitals]
    low = lax.broadcasted_iota(jnp.int32, (orbitals, LANES), 1) < orbitals - LANES
    return full_real[:, :LANES], full_imag[:, :LANES], jnp.where(low, full_real[:, LANES:], full_imag[:, LANES:])


def kernel(
    n, slabs, rows, pitch,
    green, couple, sigma, screened, inverse,
    recv2,
    green_v, couple_v, sigma_v, ahead_v, screened_v, inverse_v,
    lines, lags, total, term, send1, recv1, send2,
    local_sem, slab_send, slab_recv, send1_sem, recv1_sem, send2_sem, recv2_sem,
):
    me = lax.axis_index("energy")
    block = lax.axis_index("slab")
    orbitals = green_v.shape[1]
    length = screened_v.shape[1]
    lag_rows = n * pitch
    tail = orbitals - LANES

    barrier = pltpu.get_barrier_semaphore()

    def greet(step, _):
        pl.semaphore_signal(barrier, inc=1, device_id=(lax.rem(me + step, n), block), device_id_type=MESH)
        return 0

    @pl.when(block > 0)
    def _():
        pl.semaphore_signal(barrier, inc=1, device_id=(me, block - 1), device_id_type=MESH)

    @pl.when(block < slabs - 1)
    def _():
        pl.semaphore_signal(barrier, inc=1, device_id=(me, block + 1), device_id_type=MESH)

    lax.fori_loop(1, n, greet, 0)

    pairs = (
        (green.at[0, 0], green_v), (sigma.at[0, 0], sigma_v), (couple.at[0, 0], couple_v),
        (screened.at[0], screened_v), (inverse, inverse_v),
    )
    loads = [pltpu.make_async_copy(src, dst, local_sem.at[i]) for i, (src, dst) in enumerate(pairs)]
    for load in loads:
        load.start()

    def everyone_is_here():
        pl.semaphore_wait(barrier, n - 1 + (block > 0).astype(jnp.int32) + (block < slabs - 1).astype(jnp.int32))

    def to_block_before():
        return pltpu.make_async_remote_copy(
            src_ref=sigma.at[0, 0], dst_ref=ahead_v, send_sem=slab_send, recv_sem=slab_recv,
            device_id=(me, lax.max(block - 1, 0)), device_id_type=MESH,
        )

    @pl.when(block > 0)
    def _():
        everyone_is_here()
        to_block_before().start()

    for load in loads[:2]:
        load.wait()
    for group, value in enumerate(sandwich(green_v, sigma_v)):
        term[:orbitals, group * LANES:(group + 1) * LANES] = value
    term[orbitals:] = jnp.zeros((pitch, 3 * LANES), jnp.float32)
    loads[2].wait()

    @pl.when(block == 0)
    def _():
        everyone_is_here()

    @pl.when(block < slabs - 1)
    def _():
        to_block_before().wait_recv()
        for group, value in enumerate(sandwich(couple_v, ahead_v)):
            term[:orbitals, group * LANES:(group + 1) * LANES] += value

    for owner in range(n):
        send1[owner * pitch:(owner + 1) * pitch] = term[owner * rows:owner * rows + pitch].astype(jnp.bfloat16)

    def at(ref, index):
        return ref.at[pl.ds(pl.multiple_of(index * pitch, pitch), pitch)]

    def copy(src, dst, send_sem, recv_sem, peer, slot):
        return pltpu.make_async_remote_copy(
            src_ref=at(src, peer), dst_ref=at(dst, slot), send_sem=send_sem.at[peer], recv_sem=recv_sem.at[slot],
            device_id=(peer, block), device_id_type=MESH,
        )

    def each(act):
        def body(step, _):
            act(step)
            return 0

        lax.fori_loop(1, n, body, 0)

    first = (send1, recv1, send1_sem, recv1_sem)
    second = (send2, recv2, send2_sem, recv2_sem)

    def behind(step):
        return lax.rem(me + n - step, n)

    def ahead(step):
        return lax.rem(me + step, n)

    each(lambda step: copy(*first, ahead(step), me).start())

    loads[3].wait()
    for row in range(rows):
        where = pl.ds(row * length, length)
        for part in range(2):
            line = screened_v[part, :, row * orbitals:(row + 1) * orbitals].astype(jnp.float32)
            last = line[:, LANES:]
            lines[where, part * LANES:(part + 1) * LANES] = line[:, :LANES].astype(jnp.bfloat16)
            lines[where, (part + 2) * LANES:(part + 3) * LANES] = jnp.concatenate([last, last], axis=1).astype(jnp.bfloat16)
    loads[4].wait()
    waves = mul(inverse_v[:2 * lag_rows], lines[...]) + mul(inverse_v[2 * lag_rows:], lines[...])
    cosine, sine = waves[:lag_rows], waves[lag_rows:]
    for group in range(0, 4, 2):
        real, imag = (slice(part * LANES, (part + 1) * LANES) for part in (group, group + 1))
        shape = (n, pitch, LANES)
        lags[n - 1:, :, real] = (cosine[:, real] - sine[:, imag]).reshape(shape)
        lags[n - 1:, :, imag] = (cosine[:, imag] + sine[:, real]).reshape(shape)
        back_real = (cosine[:, real] + sine[:, imag]).reshape(shape)
        back_imag = (cosine[:, imag] - sine[:, real]).reshape(shape)
        for lag in range(1, n):
            lags[n - 1 - lag, :, real] = back_real[lag]
            lags[n - 1 - lag, :, imag] = back_imag[lag]

    sign = jnp.where(lax.broadcasted_iota(jnp.int32, (pitch, LANES), 1) < tail, -1.0, 1.0)
    parts = tuple(slice(part * LANES, (part + 1) * LANES) for part in range(4))

    def take(source, buffer):
        rows_of = buffer[pl.ds(pl.multiple_of(source * pitch, pitch), pitch), :].astype(jnp.float32)
        real, imag, mixed = rows_of[:, parts[0]], rows_of[:, parts[1]], rows_of[:, parts[2]]
        return source, real, imag, mixed, pltpu.roll(mixed, tail, 1) * sign

    def terms(taken, energy):
        source, real, imag, mixed, turned = taken
        lag = energy - source + n - 1
        by_real, by_imag, both_real, both_imag = (lags[lag, :, part] for part in parts)
        return real * by_real - imag * by_imag, real * by_imag + imag * by_real, mixed * both_real + turned * both_imag

    mine = take(me, send1)
    for energy in range(n):
        for part, value in zip(parts, terms(mine, energy)):
            total[energy, :, part] = value

    def arrived(step, _):
        source = behind(step)
        copy(*first, source, source).wait_recv()
        taken = take(source, recv1)
        for energy in range(n):
            for part, value in zip(parts, terms(taken, energy)):
                total[energy, :, part] += value
        return 0

    lax.fori_loop(1, n - 1, arrived, 0)
    source = behind(n - 1)
    copy(*first, source, source).wait_recv()
    taken = take(source, recv1)

    def finish(energy):
        where = pl.ds(pl.multiple_of(energy * pitch, pitch), pitch)
        for part, value in zip(parts, terms(taken, energy)):
            send2[where, part] = (total[energy, :, part] + value).astype(jnp.bfloat16)

    def depart(step):
        finish(ahead(step))
        copy(*second, ahead(step), me).start()

    each(depart)
    finish(me)
    keep = pltpu.make_async_copy(at(send2, me), at(recv2, me), recv2_sem.at[me])
    keep.start()
    each(lambda step: copy(*first, ahead(step), me).wait_send())

    @pl.when(block > 0)
    def _():
        to_block_before().wait_send()

    each(lambda step: copy(*second, behind(step), behind(step)).wait_recv())
    keep.wait()
    each(lambda step: copy(*second, ahead(step), me).wait_send())


def unpack(gather, packed, out):
    tail = out.shape[-1] - LANES
    result = mul(gather[...], packed[...]).astype(jnp.bfloat16)
    out[0, 0, 0, :, :LANES] = result[:, :LANES]
    out[0, 0, 1, :, :LANES] = result[:, LANES:2 * LANES]
    out[0, 0, 0, :, LANES:] = result[:, 2 * LANES:2 * LANES + tail]
    out[0, 0, 1, :, LANES:] = result[:, 2 * LANES + tail:]


def shards(n, slabs, green_block, coupling, sigma_lesser, screened):
    orbitals = green_block.shape[-1]
    length = screened.shape[2]
    rows = screened.shape[3] // orbitals
    pitch = -(-rows // PITCH) * PITCH
    assert green_block.shape[0] == 1 and length == 2 * n and rows * n == orbitals and orbitals == LANES + LANES // 2
    inverse, gather = make_tables(n, rows, pitch)
    packed = (n * pitch, 2 * orbitals)
    square = (2, orbitals, orbitals)
    bf16 = jnp.bfloat16
    returned = pl.pallas_call(
        functools.partial(kernel, n, slabs, rows, pitch),
        out_shape=jax.ShapeDtypeStruct(packed, bf16),
        in_specs=[pl.BlockSpec(memory_space=pl.ANY)] * 5,
        out_specs=pl.BlockSpec(memory_space=pl.ANY),
        scratch_shapes=[
            pltpu.VMEM(square, bf16),
            pltpu.VMEM(square, bf16),
            pltpu.VMEM(square, bf16),
            pltpu.VMEM(square, bf16),
            pltpu.VMEM(screened.shape[1:], bf16),
            pltpu.VMEM(inverse.shape, bf16),
            pltpu.VMEM((rows * length, 4 * LANES), bf16),
            pltpu.VMEM((2 * n - 1, pitch, 4 * LANES), jnp.float32),
            pltpu.VMEM((n, pitch, 3 * LANES), jnp.float32),
            pltpu.VMEM((orbitals + pitch, 3 * LANES), jnp.float32),
            pltpu.VMEM(packed, bf16),
            pltpu.VMEM(packed, bf16),
            pltpu.VMEM(packed, bf16),
            pltpu.SemaphoreType.DMA((5,)),
            pltpu.SemaphoreType.DMA,
            pltpu.SemaphoreType.DMA,
            *[pltpu.SemaphoreType.DMA((n,))] * 4,
        ],
        compiler_params=pltpu.CompilerParams(
            collective_id=0, has_side_effects=True, vmem_limit_bytes=56 * 1024 * 1024
        ),
        cost_estimate=pl.CostEstimate(flops=10**9, bytes_accessed=4 * 10**6, transcendentals=0),
        name="self_energy",
    )(green_block, coupling, sigma_lesser, screened, jnp.asarray(inverse))
    return pl.pallas_call(
        unpack,
        out_shape=jax.ShapeDtypeStruct(green_block.shape, bf16),
        in_specs=[pl.BlockSpec(memory_space=pltpu.VMEM)] * 2,
        out_specs=pl.BlockSpec(memory_space=pltpu.VMEM),
        name="unpack",
    )(jnp.asarray(gather), returned)


def solution(mesh):
    placed = (
        P("energy", "slab", None, None, None),
        P("energy", "slab", None, None, None),
        P("energy", "slab", None, None, None),
        P("slab", None, None, "energy"),
    )
    return jax.shard_map(
        functools.partial(shards, mesh.shape["energy"], mesh.shape["slab"]),
        mesh=mesh,
        in_specs=placed,
        out_specs=P("energy", "slab", None, None, None),
        check_vma=False,
    )
```

```python
import functools

import jax
import jax.numpy as jnp
import ml_dtypes
import numpy as np
from jax import lax
from jax.experimental import pallas as pl
from jax.experimental.pallas import tpu as pltpu
from jax.sharding import PartitionSpec as P

MESH = pl.DeviceIdType.MESH
LANES = 128
PITCH = 16


def split(table):
    high = table.astype(ml_dtypes.bfloat16)
    low = (table - high.astype(np.float64)).astype(ml_dtypes.bfloat16)
    return high, low


def make_tables(count, rows, pitch):
    length = 2 * count
    phases = np.outer(np.arange(count), np.arange(length)) % length
    angles = phases * (2.0 * np.pi / length)
    same = np.zeros((pitch, rows))
    same[np.arange(rows), np.arange(rows)] = 1.0
    high, low = [], []
    for table in (np.cos(angles), np.sin(angles)):
        wide = np.einsum("dk,sr->dsrk", table / length, same).reshape(count * pitch, rows * length)
        for part, into in zip(split(wide), (high, low)):
            into.append(part)
    gather = np.zeros((count * rows, count * pitch), ml_dtypes.bfloat16)
    for owner in range(count):
        for row in range(rows):
            gather[owner * rows + row, owner * pitch + row] = 1.0
    return np.concatenate(high + low, axis=0), gather


def mul(first, second):
    return jnp.dot(first, second, preferred_element_type=jnp.float32)


def mul_t(first, second):
    return lax.dot_general(first, second, (((1,), (1,)), ((), ())), preferred_element_type=jnp.float32)


def sandwich(outer, inner, ready=lambda part: None):
    orbitals = outer.shape[1]
    stacked = outer[...].reshape(2 * orbitals, orbitals)
    ready(0)
    by_real = mul(stacked, inner[0])
    ready(1)
    by_imag = mul(stacked, inner[1])
    half_real = by_real[:orbitals] - by_imag[orbitals:]
    half_imag = by_imag[:orbitals] + by_real[orbitals:]
    half = jnp.concatenate([half_real.astype(jnp.bfloat16), half_imag.astype(jnp.bfloat16)], axis=0)
    with_real = mul_t(half, jnp.concatenate([outer[0], outer[0, LANES:]], axis=0))
    with_imag = mul_t(half, jnp.concatenate([outer[1], outer[1, LANES:]], axis=0))
    full_real = with_real[:orbitals] + with_imag[orbitals:]
    full_imag = with_real[orbitals:] - with_imag[:orbitals]
    low = lax.broadcasted_iota(jnp.int32, (orbitals, LANES), 1) < orbitals - LANES
    return full_real[:, :LANES], full_imag[:, :LANES], jnp.where(low, full_real[:, LANES:], full_imag[:, LANES:])


def kernel(
    n, slabs, rows, pitch,
    green, couple, sigma, screened, inverse,
    recv2,
    green_v, couple_v, sigma_v, ahead_v, screened_v, inverse_v,
    lines, lags, total, term, send1, recv1, send2,
    local_sem, slab_send, slab_recv, paired, send1_sem, recv1_sem, send2_sem, recv2_sem,
):
    me = lax.axis_index("energy")
    block = lax.axis_index("slab")
    orbitals = green_v.shape[1]
    length = screened_v.shape[1]
    lag_rows = n * pitch
    tail = orbitals - LANES

    barrier = pltpu.get_barrier_semaphore()

    def signal(energy, slab, semaphore=barrier):
        pl.semaphore_signal(semaphore, inc=1, device_id=(energy, slab), device_id_type=MESH)

    def greet_group():
        def body(step, _):
            signal(lax.rem(me + step, n), block)
            return 0

        lax.fori_loop(1, n, body, 0)

    if slabs == 2:
        @pl.when(block == 0)
        def _():
            signal(me, 1)
    else:
        @pl.when(block > 0)
        def _():
            signal(me, block - 1)

        @pl.when(block < slabs - 1)
        def _():
            signal(me, block + 1)

        greet_group()

    pairs = (
        (green.at[0, 0], green_v), (sigma.at[0, 0], sigma_v), (couple.at[0, 0], couple_v),
        (screened.at[0], screened_v), (inverse, inverse_v),
    )
    loads = [pltpu.make_async_copy(src, dst, local_sem.at[i]) for i, (src, dst) in enumerate(pairs)]
    for load in loads:
        load.start()

    half = orbitals // 2

    def to_block_before(part):
        copies = []
        for piece in range(2):
            where = pl.ds(piece * half, half)
            copies.append(pltpu.make_async_remote_copy(
                src_ref=sigma_v.at[part, where], dst_ref=ahead_v.at[part, where],
                send_sem=slab_send.at[2 * part + piece], recv_sem=slab_recv.at[2 * part + piece],
                device_id=(me, lax.max(block - 1, 0)), device_id_type=MESH,
            ))
        return copies

    def send_sigma():
        for part in range(2):
            for piece in to_block_before(part):
                piece.start()

    loads[0].wait()
    loads[1].wait()
    if slabs == 2:
        @pl.when(block == 1)
        def _():
            pl.semaphore_wait(barrier, 1)
            signal(me, 0, paired)
            send_sigma()

        @pl.when(block == 0)
        def _():
            pl.semaphore_wait(paired, 1)
            greet_group()
    else:
        pl.semaphore_wait(barrier, n - 1 + (block > 0).astype(jnp.int32) + (block < slabs - 1).astype(jnp.int32))

        @pl.when(block > 0)
        def _():
            send_sigma()

    for group, value in enumerate(sandwich(green_v, sigma_v)):
        term[:orbitals, group * LANES:(group + 1) * LANES] = value
    term[orbitals:] = jnp.zeros((pitch, 3 * LANES), jnp.float32)
    loads[2].wait()

    if slabs == 2:
        @pl.when(block == 0)
        def _():
            pl.semaphore_wait(barrier, n - 1)
            signal(me, 1)

        @pl.when(block == 1)
        def _():
            pl.semaphore_wait(barrier, 1)

    def sigma_is_here(part):
        for piece in to_block_before(part):
            piece.wait_recv()

    @pl.when(block < slabs - 1)
    def _():
        for group, value in enumerate(sandwich(couple_v, ahead_v, sigma_is_here)):
            term[:orbitals, group * LANES:(group + 1) * LANES] += value

    for owner in range(n):
        send1[owner * pitch:(owner + 1) * pitch] = term[owner * rows:owner * rows + pitch].astype(jnp.bfloat16)

    def at(ref, index):
        return ref.at[pl.ds(pl.multiple_of(index * pitch, pitch), pitch)]

    def copy(src, dst, send_sem, recv_sem, peer, slot):
        return pltpu.make_async_remote_copy(
            src_ref=at(src, peer), dst_ref=at(dst, slot), send_sem=send_sem.at[peer], recv_sem=recv_sem.at[slot],
            device_id=(peer, block), device_id_type=MESH,
        )

    def each(act):
        def body(step, _):
            act(step)
            return 0

        lax.fori_loop(1, n, body, 0)

    first = (send1, recv1, send1_sem, recv1_sem)
    second = (send2, recv2, send2_sem, recv2_sem)

    def behind(step):
        return lax.rem(me + n - step, n)

    def ahead(step):
        return lax.rem(me + step, n)

    each(lambda step: copy(*first, ahead(step), me).start())

    loads[3].wait()
    for row in range(rows):
        where = pl.ds(row * length, length)
        for part in range(2):
            line = screened_v[part, :, row * orbitals:(row + 1) * orbitals].astype(jnp.float32)
            last = line[:, LANES:]
            lines[where, part * LANES:(part + 1) * LANES] = line[:, :LANES].astype(jnp.bfloat16)
            lines[where, (part + 2) * LANES:(part + 3) * LANES] = jnp.concatenate([last, last], axis=1).astype(jnp.bfloat16)
    loads[4].wait()
    waves = mul(inverse_v[:2 * lag_rows], lines[...]) + mul(inverse_v[2 * lag_rows:], lines[...])
    cosine, sine = waves[:lag_rows], waves[lag_rows:]
    for group in range(0, 4, 2):
        real, imag = (slice(part * LANES, (part + 1) * LANES) for part in (group, group + 1))
        shape = (n, pitch, LANES)
        lags[n - 1:, :, real] = (cosine[:, real] - sine[:, imag]).reshape(shape)
        lags[n - 1:, :, imag] = (cosine[:, imag] + sine[:, real]).reshape(shape)
        back_real = (cosine[:, real] + sine[:, imag]).reshape(shape)
        back_imag = (cosine[:, imag] - sine[:, real]).reshape(shape)
        for lag in range(1, n):
            lags[n - 1 - lag, :, real] = back_real[lag]
            lags[n - 1 - lag, :, imag] = back_imag[lag]

    sign = jnp.where(lax.broadcasted_iota(jnp.int32, (pitch, LANES), 1) < tail, -1.0, 1.0)
    parts = tuple(slice(part * LANES, (part + 1) * LANES) for part in range(4))

    def take(source, buffer):
        rows_of = buffer[pl.ds(pl.multiple_of(source * pitch, pitch), pitch), :].astype(jnp.float32)
        real, imag, mixed = rows_of[:, parts[0]], rows_of[:, parts[1]], rows_of[:, parts[2]]
        return source, real, imag, mixed, pltpu.roll(mixed, tail, 1) * sign

    def terms(taken, energy):
        source, real, imag, mixed, turned = taken
        lag = energy - source + n - 1
        by_real, by_imag, both_real, both_imag = (lags[lag, :, part] for part in parts)
        return real * by_real - imag * by_imag, real * by_imag + imag * by_real, mixed * both_real + turned * both_imag

    mine = take(me, send1)
    for energy in range(n):
        for part, value in zip(parts, terms(mine, energy)):
            total[energy, :, part] = value

    def arrived(step, _):
        source = behind(step)
        copy(*first, source, source).wait_recv()
        taken = take(source, recv1)
        for energy in range(n):
            for part, value in zip(parts, terms(taken, energy)):
                total[energy, :, part] += value
        return 0

    lax.fori_loop(1, n - 1, arrived, 0)
    source = behind(n - 1)
    copy(*first, source, source).wait_recv()
    taken = take(source, recv1)

    def finish(energy):
        where = pl.ds(pl.multiple_of(energy * pitch, pitch), pitch)
        for part, value in zip(parts, terms(taken, energy)):
            send2[where, part] = (total[energy, :, part] + value).astype(jnp.bfloat16)

    def depart(step):
        finish(ahead(step))
        copy(*second, ahead(step), me).start()

    each(depart)
    finish(me)
    keep = pltpu.make_async_copy(at(send2, me), at(recv2, me), recv2_sem.at[me])
    keep.start()
    each(lambda step: copy(*first, ahead(step), me).wait_send())

    @pl.when(block > 0)
    def _():
        for part in range(2):
            for piece in to_block_before(part):
                piece.wait_send()

    each(lambda step: copy(*second, behind(step), behind(step)).wait_recv())
    keep.wait()
    each(lambda step: copy(*second, ahead(step), me).wait_send())


def unpack(gather, packed, out):
    tail = out.shape[-1] - LANES
    result = mul(gather[...], packed[...]).astype(jnp.bfloat16)
    out[0, 0, 0, :, :LANES] = result[:, :LANES]
    out[0, 0, 1, :, :LANES] = result[:, LANES:2 * LANES]
    out[0, 0, 0, :, LANES:] = result[:, 2 * LANES:2 * LANES + tail]
    out[0, 0, 1, :, LANES:] = result[:, 2 * LANES + tail:]


def shards(n, slabs, green_block, coupling, sigma_lesser, screened):
    orbitals = green_block.shape[-1]
    length = screened.shape[2]
    rows = screened.shape[3] // orbitals
    pitch = -(-rows // PITCH) * PITCH
    assert green_block.shape[0] == 1 and length == 2 * n and rows * n == orbitals and orbitals == LANES + LANES // 2
    inverse, gather = make_tables(n, rows, pitch)
    packed = (n * pitch, 2 * orbitals)
    square = (2, orbitals, orbitals)
    bf16 = jnp.bfloat16
    returned = pl.pallas_call(
        functools.partial(kernel, n, slabs, rows, pitch),
        out_shape=jax.ShapeDtypeStruct(packed, bf16),
        in_specs=[pl.BlockSpec(memory_space=pl.ANY)] * 5,
        out_specs=pl.BlockSpec(memory_space=pl.ANY),
        scratch_shapes=[
            pltpu.VMEM(square, bf16),
            pltpu.VMEM(square, bf16),
            pltpu.VMEM(square, bf16),
            pltpu.VMEM(square, bf16),
            pltpu.VMEM(screened.shape[1:], bf16),
            pltpu.VMEM(inverse.shape, bf16),
            pltpu.VMEM((rows * length, 4 * LANES), bf16),
            pltpu.VMEM((2 * n - 1, pitch, 4 * LANES), jnp.float32),
            pltpu.VMEM((n, pitch, 3 * LANES), jnp.float32),
            pltpu.VMEM((orbitals + pitch, 3 * LANES), jnp.float32),
            pltpu.VMEM(packed, bf16),
            pltpu.VMEM(packed, bf16),
            pltpu.VMEM(packed, bf16),
            pltpu.SemaphoreType.DMA((5,)),
            pltpu.SemaphoreType.DMA((4,)),
            pltpu.SemaphoreType.DMA((4,)),
            pltpu.SemaphoreType.REGULAR,
            *[pltpu.SemaphoreType.DMA((n,))] * 4,
        ],
        compiler_params=pltpu.CompilerParams(
            collective_id=0, has_side_effects=True, vmem_limit_bytes=56 * 1024 * 1024
        ),
        cost_estimate=pl.CostEstimate(flops=10**9, bytes_accessed=4 * 10**6, transcendentals=0),
        name="self_energy",
    )(green_block, coupling, sigma_lesser, screened, jnp.asarray(inverse))
    return pl.pallas_call(
        unpack,
        out_shape=jax.ShapeDtypeStruct(green_block.shape, bf16),
        in_specs=[pl.BlockSpec(memory_space=pltpu.VMEM)] * 2,
        out_specs=pl.BlockSpec(memory_space=pltpu.VMEM),
        name="unpack",
    )(jnp.asarray(gather), returned)


def solution(mesh):
    placed = (
        P("energy", "slab", None, None, None),
        P("energy", "slab", None, None, None),
        P("energy", "slab", None, None, None),
        P("slab", None, None, "energy"),
    )
    return jax.shard_map(
        functools.partial(shards, mesh.shape["energy"], mesh.shape["slab"]),
        mesh=mesh,
        in_specs=placed,
        out_specs=P("energy", "slab", None, None, None),
        check_vma=False,
    )
```

```python
import functools

import jax
import jax.numpy as jnp
import ml_dtypes
import numpy as np
from jax import lax
from jax.experimental import pallas as pl
from jax.experimental.pallas import tpu as pltpu
from jax.sharding import PartitionSpec as P

MESH = pl.DeviceIdType.MESH
LANES = 128
PITCH = 16


def split(table):
    high = table.astype(ml_dtypes.bfloat16)
    low = (table - high.astype(np.float64)).astype(ml_dtypes.bfloat16)
    return high, low


def make_tables(count, rows, pitch):
    length = 2 * count
    phases = np.outer(np.arange(count), np.arange(length)) % length
    angles = phases * (2.0 * np.pi / length)
    same = np.zeros((pitch, rows))
    same[np.arange(rows), np.arange(rows)] = 1.0
    high, low = [], []
    for table in (np.cos(angles), np.sin(angles)):
        wide = np.einsum("dk,sr->dsrk", table / length, same).reshape(count * pitch, rows * length)
        for part, into in zip(split(wide), (high, low)):
            into.append(part)
    gather = np.zeros((count * rows, count * pitch), ml_dtypes.bfloat16)
    for owner in range(count):
        for row in range(rows):
            gather[owner * rows + row, owner * pitch + row] = 1.0
    return np.concatenate(high + low, axis=0), gather


def mul(first, second):
    return jnp.dot(first, second, preferred_element_type=jnp.float32)


def mul_t(first, second):
    return lax.dot_general(first, second, (((1,), (1,)), ((), ())), preferred_element_type=jnp.float32)


def sandwich(outer, inner):
    orbitals = outer.shape[1]
    stacked = outer[...].reshape(2 * orbitals, orbitals)
    by_real = mul(stacked, inner[0])
    by_imag = mul(stacked, inner[1])
    half_real = by_real[:orbitals] - by_imag[orbitals:]
    half_imag = by_imag[:orbitals] + by_real[orbitals:]
    half = jnp.concatenate([half_real.astype(jnp.bfloat16), half_imag.astype(jnp.bfloat16)], axis=0)
    with_real = mul_t(half, jnp.concatenate([outer[0], outer[0, LANES:]], axis=0))
    with_imag = mul_t(half, jnp.concatenate([outer[1], outer[1, LANES:]], axis=0))
    full_real = with_real[:orbitals] + with_imag[orbitals:]
    full_imag = with_real[orbitals:] - with_imag[:orbitals]
    low = lax.broadcasted_iota(jnp.int32, (orbitals, LANES), 1) < orbitals - LANES
    return full_real[:, :LANES], full_imag[:, :LANES], jnp.where(low, full_real[:, LANES:], full_imag[:, LANES:])


def kernel(
    n, slabs, rows, pitch,
    green, couple, sigma, screened, inverse,
    recv2,
    outer_v, inner_v, screened_v, inverse_v,
    lines, lags, total, term, send1, recv1, send2,
    local_sem, slab_send, slab_recv, send1_sem, recv1_sem, send2_sem, recv2_sem,
):
    me = lax.axis_index("energy")
    block = lax.axis_index("slab")
    orbitals = outer_v.shape[2]
    length = screened_v.shape[1]
    lag_rows = n * pitch
    tail = orbitals - LANES

    pairs = (
        (green.at[0, 0], outer_v.at[0]), (sigma.at[0, 0], inner_v.at[0]), (couple.at[0, 0], outer_v.at[1]),
        (screened.at[0], screened_v), (inverse, inverse_v),
    )
    loads = [pltpu.make_async_copy(src, dst, local_sem.at[i]) for i, (src, dst) in enumerate(pairs)]
    for load in loads[:2]:
        load.start()

    barrier = pltpu.get_barrier_semaphore()

    def greet(step, _):
        pl.semaphore_signal(barrier, inc=1, device_id=(lax.rem(me + step, n), block), device_id_type=MESH)
        return 0

    @pl.when(block > 0)
    def _():
        pl.semaphore_signal(barrier, inc=1, device_id=(me, block - 1), device_id_type=MESH)

    @pl.when(block < slabs - 1)
    def _():
        pl.semaphore_signal(barrier, inc=1, device_id=(me, block + 1), device_id_type=MESH)

    lax.fori_loop(1, n, greet, 0)

    def everyone_is_here():
        pl.semaphore_wait(barrier, n - 1 + (block > 0).astype(jnp.int32) + (block < slabs - 1).astype(jnp.int32))

    def to_block_before():
        return pltpu.make_async_remote_copy(
            src_ref=sigma.at[0, 0], dst_ref=inner_v.at[1], send_sem=slab_send, recv_sem=slab_recv,
            device_id=(me, lax.max(block - 1, 0)), device_id_type=MESH,
        )

    term[...] = jnp.zeros_like(term)
    loads[0].wait()
    loads[1].wait()
    for load in loads[2:]:
        load.start()

    @pl.when(block > 0)
    def _():
        everyone_is_here()
        to_block_before().start()

    def add_term(index, _):
        @pl.when(index == 1)
        def _():
            loads[2].wait()
            to_block_before().wait_recv()

        for group, value in enumerate(sandwich(outer_v.at[index], inner_v.at[index])):
            term[:orbitals, group * LANES:(group + 1) * LANES] += value
        return 0

    lax.fori_loop(0, 1 + (block < slabs - 1).astype(jnp.int32), add_term, 0)

    @pl.when(block == slabs - 1)
    def _():
        loads[2].wait()

    @pl.when(block == 0)
    def _():
        everyone_is_here()

    for owner in range(n):
        send1[owner * pitch:(owner + 1) * pitch] = term[owner * rows:owner * rows + pitch].astype(jnp.bfloat16)

    def at(ref, index):
        return ref.at[pl.ds(pl.multiple_of(index * pitch, pitch), pitch)]

    def copy(src, dst, send_sem, recv_sem, peer, slot):
        return pltpu.make_async_remote_copy(
            src_ref=at(src, peer), dst_ref=at(dst, slot), send_sem=send_sem.at[peer], recv_sem=recv_sem.at[slot],
            device_id=(peer, block), device_id_type=MESH,
        )

    def each(act):
        def body(step, _):
            act(step)
            return 0

        lax.fori_loop(1, n, body, 0)

    first = (send1, recv1, send1_sem, recv1_sem)
    second = (send2, recv2, send2_sem, recv2_sem)

    def behind(step):
        return lax.rem(me + n - step, n)

    def ahead(step):
        return lax.rem(me + step, n)

    each(lambda step: copy(*first, ahead(step), me).start())
    own = pltpu.make_async_copy(at(send1, me), at(recv1, me), recv1_sem.at[me])
    own.start()

    loads[3].wait()
    for row in range(rows):
        where = pl.ds(row * length, length)
        for part in range(2):
            line = screened_v[part, :, row * orbitals:(row + 1) * orbitals].astype(jnp.float32)
            last = line[:, LANES:]
            lines[where, part * LANES:(part + 1) * LANES] = line[:, :LANES].astype(jnp.bfloat16)
            lines[where, (part + 2) * LANES:(part + 3) * LANES] = jnp.concatenate([last, last], axis=1).astype(jnp.bfloat16)
    loads[4].wait()
    count = min(n, 8)

    def make_lags(chunk, _):
        def waves(kind):
            high = pl.ds(pl.multiple_of(kind * lag_rows + chunk * count * pitch, count * pitch), count * pitch)
            low = pl.ds(pl.multiple_of((kind + 2) * lag_rows + chunk * count * pitch, count * pitch), count * pitch)
            return mul(inverse_v[high], lines[...]) + mul(inverse_v[low], lines[...])

        cosine, sine = waves(0), waves(1)
        for group in range(0, 4, 2):
            real, imag = (slice(part * LANES, (part + 1) * LANES) for part in (group, group + 1))
            for lag in range(count):
                own = slice(lag * pitch, (lag + 1) * pitch)
                up = n - 1 + chunk * count + lag
                down = n - 1 - chunk * count - lag
                lags[down, :, real] = cosine[own, real] + sine[own, imag]
                lags[down, :, imag] = cosine[own, imag] - sine[own, real]
                lags[up, :, real] = cosine[own, real] - sine[own, imag]
                lags[up, :, imag] = cosine[own, imag] + sine[own, real]
        return 0

    lax.fori_loop(0, n // count, make_lags, 0)

    sign = jnp.where(lax.broadcasted_iota(jnp.int32, (pitch, LANES), 1) < tail, -1.0, 1.0)
    parts = tuple(slice(part * LANES, (part + 1) * LANES) for part in range(4))

    def take(source, buffer):
        rows_of = buffer[pl.ds(pl.multiple_of(source * pitch, pitch), pitch), :].astype(jnp.float32)
        real, imag, mixed = rows_of[:, parts[0]], rows_of[:, parts[1]], rows_of[:, parts[2]]
        return source, real, imag, mixed, pltpu.roll(mixed, tail, 1) * sign

    def terms(taken, energy):
        source, real, imag, mixed, turned = taken
        lag = energy - source + n - 1
        by_real, by_imag, both_real, both_imag = (lags[lag, :, part] for part in parts)
        return real * by_real - imag * by_imag, real * by_imag + imag * by_real, mixed * both_real + turned * both_imag

    def clear(energy, _):
        total[energy] = jnp.zeros((pitch, 3 * LANES), jnp.float32)
        return 0

    lax.fori_loop(0, n, clear, 0)
    own.wait()

    def arrived(step, _):
        source = behind(step)

        @pl.when(step > 0)
        def _():
            copy(*first, source, source).wait_recv()

        taken = take(source, recv1)
        for energy in range(n):
            for part, value in zip(parts, terms(taken, energy)):
                total[energy, :, part] += value
        return 0

    lax.fori_loop(0, n - 1, arrived, 0)
    source = behind(n - 1)
    copy(*first, source, source).wait_recv()
    taken = take(source, recv1)

    def finish(energy):
        where = pl.ds(pl.multiple_of(energy * pitch, pitch), pitch)
        for part, value in zip(parts, terms(taken, energy)):
            send2[where, part] = (total[energy, :, part] + value).astype(jnp.bfloat16)

    def depart(step):
        finish(ahead(step))
        copy(*second, ahead(step), me).start()

    each(depart)
    finish(me)
    keep = pltpu.make_async_copy(at(send2, me), at(recv2, me), recv2_sem.at[me])
    keep.start()
    each(lambda step: copy(*first, ahead(step), me).wait_send())

    @pl.when(block > 0)
    def _():
        to_block_before().wait_send()

    each(lambda step: copy(*second, behind(step), behind(step)).wait_recv())
    keep.wait()
    each(lambda step: copy(*second, ahead(step), me).wait_send())


def unpack(gather, packed, out):
    tail = out.shape[-1] - LANES
    result = mul(gather[...], packed[...]).astype(jnp.bfloat16)
    out[0, 0, 0, :, :LANES] = result[:, :LANES]
    out[0, 0, 1, :, :LANES] = result[:, LANES:2 * LANES]
    out[0, 0, 0, :, LANES:] = result[:, 2 * LANES:2 * LANES + tail]
    out[0, 0, 1, :, LANES:] = result[:, 2 * LANES + tail:]


def shards(n, slabs, green_block, coupling, sigma_lesser, screened):
    orbitals = green_block.shape[-1]
    length = screened.shape[2]
    rows = screened.shape[3] // orbitals
    pitch = -(-rows // PITCH) * PITCH
    assert green_block.shape[0] == 1 and length == 2 * n and rows * n == orbitals and orbitals == LANES + LANES // 2
    inverse, gather = make_tables(n, rows, pitch)
    packed = (n * pitch, 2 * orbitals)
    square = (2, orbitals, orbitals)
    bf16 = jnp.bfloat16
    returned = pl.pallas_call(
        functools.partial(kernel, n, slabs, rows, pitch),
        out_shape=jax.ShapeDtypeStruct(packed, bf16),
        in_specs=[pl.BlockSpec(memory_space=pl.ANY)] * 5,
        out_specs=pl.BlockSpec(memory_space=pl.ANY),
        scratch_shapes=[
            pltpu.VMEM((2, *square), bf16),
            pltpu.VMEM((2, *square), bf16),
            pltpu.VMEM(screened.shape[1:], bf16),
            pltpu.VMEM(inverse.shape, bf16),
            pltpu.VMEM((rows * length, 4 * LANES), bf16),
            pltpu.VMEM((2 * n - 1, pitch, 4 * LANES), jnp.float32),
            pltpu.VMEM((n, pitch, 3 * LANES), jnp.float32),
            pltpu.VMEM((orbitals + pitch, 3 * LANES), jnp.float32),
            pltpu.VMEM(packed, bf16),
            pltpu.VMEM(packed, bf16),
            pltpu.VMEM(packed, bf16),
            pltpu.SemaphoreType.DMA((5,)),
            pltpu.SemaphoreType.DMA,
            pltpu.SemaphoreType.DMA,
            *[pltpu.SemaphoreType.DMA((n,))] * 4,
        ],
        compiler_params=pltpu.CompilerParams(
            collective_id=0, has_side_effects=True, vmem_limit_bytes=56 * 1024 * 1024
        ),
        cost_estimate=pl.CostEstimate(flops=10**9, bytes_accessed=4 * 10**6, transcendentals=0),
        name="self_energy",
    )(green_block, coupling, sigma_lesser, screened, jnp.asarray(inverse))
    return pl.pallas_call(
        unpack,
        out_shape=jax.ShapeDtypeStruct(green_block.shape, bf16),
        in_specs=[pl.BlockSpec(memory_space=pltpu.VMEM)] * 2,
        out_specs=pl.BlockSpec(memory_space=pltpu.VMEM),
        name="unpack",
    )(jnp.asarray(gather), returned)


def solution(mesh):
    placed = (
        P("energy", "slab", None, None, None),
        P("energy", "slab", None, None, None),
        P("energy", "slab", None, None, None),
        P("slab", None, None, "energy"),
    )
    return jax.shard_map(
        functools.partial(shards, mesh.shape["energy"], mesh.shape["slab"]),
        mesh=mesh,
        in_specs=placed,
        out_specs=P("energy", "slab", None, None, None),
        check_vma=False,
    )
```

```python
import functools

import jax
import jax.numpy as jnp
import ml_dtypes
import numpy as np
from jax import lax
from jax.experimental import pallas as pl
from jax.experimental.pallas import tpu as pltpu
from jax.sharding import PartitionSpec as P

MESH = pl.DeviceIdType.MESH
LANES = 128
PITCH = 16


def split(table):
    high = table.astype(ml_dtypes.bfloat16)
    low = (table - high.astype(np.float64)).astype(ml_dtypes.bfloat16)
    return high, low


def make_tables(count, rows, pitch):
    length = 2 * count
    phases = np.outer(np.arange(count), np.arange(length)) % length
    angles = phases * (2.0 * np.pi / length)
    same = np.zeros((pitch, rows))
    same[np.arange(rows), np.arange(rows)] = 1.0
    high, low = [], []
    for table in (np.cos(angles), np.sin(angles)):
        wide = np.einsum("dk,sr->dsrk", table / length, same).reshape(count * pitch, rows * length)
        for part, into in zip(split(wide), (high, low)):
            into.append(part)
    gather = np.zeros((count * rows, count * pitch), ml_dtypes.bfloat16)
    for owner in range(count):
        for row in range(rows):
            gather[owner * rows + row, owner * pitch + row] = 1.0
    return np.concatenate(high + low, axis=0), gather


def mul(first, second):
    return jnp.dot(first, second, preferred_element_type=jnp.float32)


def mul_t(first, second):
    return lax.dot_general(first, second, (((1,), (1,)), ((), ())), preferred_element_type=jnp.float32)


def sandwich(outer, inner):
    orbitals = outer.shape[1]
    stacked = outer[...].reshape(2 * orbitals, orbitals)
    by_real = mul(stacked, inner[0])
    by_imag = mul(stacked, inner[1])
    half_real = by_real[:orbitals] - by_imag[orbitals:]
    half_imag = by_imag[:orbitals] + by_real[orbitals:]
    half = jnp.concatenate([half_real.astype(jnp.bfloat16), half_imag.astype(jnp.bfloat16)], axis=0)
    with_real = mul_t(half, jnp.concatenate([outer[0], outer[0, LANES:]], axis=0))
    with_imag = mul_t(half, jnp.concatenate([outer[1], outer[1, LANES:]], axis=0))
    full_real = with_real[:orbitals] + with_imag[orbitals:]
    full_imag = with_real[orbitals:] - with_imag[:orbitals]
    low = lax.broadcasted_iota(jnp.int32, (orbitals, LANES), 1) < orbitals - LANES
    return full_real[:, :LANES], full_imag[:, :LANES], jnp.where(low, full_real[:, LANES:], full_imag[:, LANES:])


def kernel(
    n, slabs, rows, pitch,
    green, couple, sigma, screened, inverse,
    recv2,
    outer_v, inner_v, sigma_out, sigma_in, screened_v, inverse_v,
    lines, lags, total, term, send1, recv1, send2,
    local_sem, slab_send, slab_recv, send1_sem, recv1_sem, send2_sem, recv2_sem,
):
    me = lax.axis_index("energy")
    block = lax.axis_index("slab")
    orbitals = outer_v.shape[2]
    length = screened_v.shape[1]
    lag_rows = n * pitch
    tail = orbitals - LANES

    pairs = (
        (green.at[0, 0], outer_v.at[0]), (sigma.at[0, 0], inner_v.at[0]), (couple.at[0, 0], outer_v.at[1]),
        (screened.at[0], screened_v), (inverse, inverse_v),
    )
    loads = [pltpu.make_async_copy(src, dst, local_sem.at[i]) for i, (src, dst) in enumerate(pairs)]
    for load in loads[:2]:
        load.start()

    barrier = pltpu.get_barrier_semaphore()

    def greet(step, _):
        pl.semaphore_signal(barrier, inc=1, device_id=(lax.rem(me + step, n), block), device_id_type=MESH)
        return 0

    @pl.when(block > 0)
    def _():
        pl.semaphore_signal(barrier, inc=1, device_id=(me, block - 1), device_id_type=MESH)

    @pl.when(block < slabs - 1)
    def _():
        pl.semaphore_signal(barrier, inc=1, device_id=(me, block + 1), device_id_type=MESH)

    lax.fori_loop(1, n, greet, 0)

    def everyone_is_here():
        pl.semaphore_wait(barrier, n - 1 + (block > 0).astype(jnp.int32) + (block < slabs - 1).astype(jnp.int32))

    def to_block_before():
        return pltpu.make_async_remote_copy(
            src_ref=sigma_out, dst_ref=sigma_in, send_sem=slab_send, recv_sem=slab_recv,
            device_id=(me, lax.max(block - 1, 0)), device_id_type=MESH,
        )

    term[...] = jnp.zeros_like(term)
    loads[0].wait()
    loads[1].wait()
    for load in loads[2:]:
        load.start()

    @pl.when(block > 0)
    def _():
        tails = [inner_v[0, part, :, LANES:].astype(jnp.float32) for part in range(2)]
        sigma_out[:, :LANES] = inner_v[0, 0, :, :LANES]
        sigma_out[:, LANES:2 * LANES] = inner_v[0, 1, :, :LANES]
        sigma_out[:, 2 * LANES:] = jnp.concatenate(tails, axis=1).astype(jnp.bfloat16)
        everyone_is_here()
        to_block_before().start()

    def add_term(index, _):
        @pl.when(index == 1)
        def _():
            loads[2].wait()
            to_block_before().wait_recv()
            inner_v[1, 0, :, :LANES] = sigma_in[:, :LANES]
            inner_v[1, 1, :, :LANES] = sigma_in[:, LANES:2 * LANES]
            mixed = sigma_in[:, 2 * LANES:]
            inner_v[1, 0, :, LANES:] = mixed[:, :tail]
            inner_v[1, 1, :, LANES:] = mixed[:, tail:]

        for group, value in enumerate(sandwich(outer_v.at[index], inner_v.at[index])):
            term[:orbitals, group * LANES:(group + 1) * LANES] += value
        return 0

    lax.fori_loop(0, 1 + (block < slabs - 1).astype(jnp.int32), add_term, 0)

    @pl.when(block == slabs - 1)
    def _():
        loads[2].wait()

    @pl.when(block == 0)
    def _():
        everyone_is_here()

    for owner in range(n):
        send1[owner * pitch:(owner + 1) * pitch] = term[owner * rows:owner * rows + pitch].astype(jnp.bfloat16)

    def at(ref, index):
        return ref.at[pl.ds(pl.multiple_of(index * pitch, pitch), pitch)]

    def copy(src, dst, send_sem, recv_sem, peer, slot):
        return pltpu.make_async_remote_copy(
            src_ref=at(src, peer), dst_ref=at(dst, slot), send_sem=send_sem.at[peer], recv_sem=recv_sem.at[slot],
            device_id=(peer, block), device_id_type=MESH,
        )

    def each(act):
        def body(step, _):
            act(step)
            return 0

        lax.fori_loop(1, n, body, 0)

    first = (send1, recv1, send1_sem, recv1_sem)
    second = (send2, recv2, send2_sem, recv2_sem)

    def behind(step):
        return lax.rem(me + n - step, n)

    def ahead(step):
        return lax.rem(me + step, n)

    each(lambda step: copy(*first, ahead(step), me).start())
    own = pltpu.make_async_copy(at(send1, me), at(recv1, me), recv1_sem.at[me])
    own.start()

    loads[3].wait()
    for row in range(rows):
        where = pl.ds(row * length, length)
        for part in range(2):
            line = screened_v[part, :, row * orbitals:(row + 1) * orbitals].astype(jnp.float32)
            last = line[:, LANES:]
            lines[where, part * LANES:(part + 1) * LANES] = line[:, :LANES].astype(jnp.bfloat16)
            lines[where, (part + 2) * LANES:(part + 3) * LANES] = jnp.concatenate([last, last], axis=1).astype(jnp.bfloat16)
    loads[4].wait()
    count = min(n, 8)

    def make_lags(chunk, _):
        def waves(kind):
            high = pl.ds(pl.multiple_of(kind * lag_rows + chunk * count * pitch, count * pitch), count * pitch)
            low = pl.ds(pl.multiple_of((kind + 2) * lag_rows + chunk * count * pitch, count * pitch), count * pitch)
            return mul(inverse_v[high], lines[...]) + mul(inverse_v[low], lines[...])

        cosine, sine = waves(0), waves(1)
        for group in range(0, 4, 2):
            real, imag = (slice(part * LANES, (part + 1) * LANES) for part in (group, group + 1))
            for lag in range(count):
                own = slice(lag * pitch, (lag + 1) * pitch)
                up = n - 1 + chunk * count + lag
                down = n - 1 - chunk * count - lag
                lags[down, :, real] = cosine[own, real] + sine[own, imag]
                lags[down, :, imag] = cosine[own, imag] - sine[own, real]
                lags[up, :, real] = cosine[own, real] - sine[own, imag]
                lags[up, :, imag] = cosine[own, imag] + sine[own, real]
        return 0

    lax.fori_loop(0, n // count, make_lags, 0)

    sign = jnp.where(lax.broadcasted_iota(jnp.int32, (pitch, LANES), 1) < tail, -1.0, 1.0)
    parts = tuple(slice(part * LANES, (part + 1) * LANES) for part in range(4))

    def take(source, buffer):
        rows_of = buffer[pl.ds(pl.multiple_of(source * pitch, pitch), pitch), :].astype(jnp.float32)
        real, imag, mixed = rows_of[:, parts[0]], rows_of[:, parts[1]], rows_of[:, parts[2]]
        return source, real, imag, mixed, pltpu.roll(mixed, tail, 1) * sign

    def terms(taken, energy):
        source, real, imag, mixed, turned = taken
        lag = energy - source + n - 1
        by_real, by_imag, both_real, both_imag = (lags[lag, :, part] for part in parts)
        return real * by_real - imag * by_imag, real * by_imag + imag * by_real, mixed * both_real + turned * both_imag

    def clear(energy, _):
        total[energy] = jnp.zeros((pitch, 3 * LANES), jnp.float32)
        return 0

    lax.fori_loop(0, n, clear, 0)
    own.wait()

    def arrived(step, _):
        source = behind(step)

        @pl.when(step > 0)
        def _():
            copy(*first, source, source).wait_recv()

        taken = take(source, recv1)
        for energy in range(n):
            for part, value in zip(parts, terms(taken, energy)):
                total[energy, :, part] += value
        return 0

    lax.fori_loop(0, n - 1, arrived, 0)
    source = behind(n - 1)
    copy(*first, source, source).wait_recv()
    taken = take(source, recv1)

    def finish(energy):
        where = pl.ds(pl.multiple_of(energy * pitch, pitch), pitch)
        for part, value in zip(parts, terms(taken, energy)):
            send2[where, part] = (total[energy, :, part] + value).astype(jnp.bfloat16)

    def depart(step):
        finish(ahead(step))
        copy(*second, ahead(step), me).start()

    each(depart)
    finish(me)
    keep = pltpu.make_async_copy(at(send2, me), at(recv2, me), recv2_sem.at[me])
    keep.start()
    each(lambda step: copy(*first, ahead(step), me).wait_send())

    @pl.when(block > 0)
    def _():
        to_block_before().wait_send()

    each(lambda step: copy(*second, behind(step), behind(step)).wait_recv())
    keep.wait()
    each(lambda step: copy(*second, ahead(step), me).wait_send())


def unpack(gather, packed, out):
    tail = out.shape[-1] - LANES
    result = mul(gather[...], packed[...]).astype(jnp.bfloat16)
    out[0, 0, 0, :, :LANES] = result[:, :LANES]
    out[0, 0, 1, :, :LANES] = result[:, LANES:2 * LANES]
    out[0, 0, 0, :, LANES:] = result[:, 2 * LANES:2 * LANES + tail]
    out[0, 0, 1, :, LANES:] = result[:, 2 * LANES + tail:]


def shards(n, slabs, green_block, coupling, sigma_lesser, screened):
    orbitals = green_block.shape[-1]
    length = screened.shape[2]
    rows = screened.shape[3] // orbitals
    pitch = -(-rows // PITCH) * PITCH
    assert green_block.shape[0] == 1 and length == 2 * n and rows * n == orbitals and orbitals == LANES + LANES // 2
    inverse, gather = make_tables(n, rows, pitch)
    packed = (n * pitch, 2 * orbitals)
    square = (2, orbitals, orbitals)
    bf16 = jnp.bfloat16
    returned = pl.pallas_call(
        functools.partial(kernel, n, slabs, rows, pitch),
        out_shape=jax.ShapeDtypeStruct(packed, bf16),
        in_specs=[pl.BlockSpec(memory_space=pl.ANY)] * 5,
        out_specs=pl.BlockSpec(memory_space=pl.ANY),
        scratch_shapes=[
            pltpu.VMEM((2, *square), bf16),
            pltpu.VMEM((2, *square), bf16),
            pltpu.VMEM((orbitals, 3 * LANES), bf16),
            pltpu.VMEM((orbitals, 3 * LANES), bf16),
            pltpu.VMEM(screened.shape[1:], bf16),
            pltpu.VMEM(inverse.shape, bf16),
            pltpu.VMEM((rows * length, 4 * LANES), bf16),
            pltpu.VMEM((2 * n - 1, pitch, 4 * LANES), jnp.float32),
            pltpu.VMEM((n, pitch, 3 * LANES), jnp.float32),
            pltpu.VMEM((orbitals + pitch, 3 * LANES), jnp.float32),
            pltpu.VMEM(packed, bf16),
            pltpu.VMEM(packed, bf16),
            pltpu.VMEM(packed, bf16),
            pltpu.SemaphoreType.DMA((5,)),
            pltpu.SemaphoreType.DMA,
            pltpu.SemaphoreType.DMA,
            *[pltpu.SemaphoreType.DMA((n,))] * 4,
        ],
        compiler_params=pltpu.CompilerParams(
            collective_id=0, has_side_effects=True, vmem_limit_bytes=56 * 1024 * 1024
        ),
        cost_estimate=pl.CostEstimate(flops=10**9, bytes_accessed=4 * 10**6, transcendentals=0),
        name="self_energy",
    )(green_block, coupling, sigma_lesser, screened, jnp.asarray(inverse))
    return pl.pallas_call(
        unpack,
        out_shape=jax.ShapeDtypeStruct(green_block.shape, bf16),
        in_specs=[pl.BlockSpec(memory_space=pltpu.VMEM)] * 2,
        out_specs=pl.BlockSpec(memory_space=pltpu.VMEM),
        name="unpack",
    )(jnp.asarray(gather), returned)


def solution(mesh):
    placed = (
        P("energy", "slab", None, None, None),
        P("energy", "slab", None, None, None),
        P("energy", "slab", None, None, None),
        P("slab", None, None, "energy"),
    )
    return jax.shard_map(
        functools.partial(shards, mesh.shape["energy"], mesh.shape["slab"]),
        mesh=mesh,
        in_specs=placed,
        out_specs=P("energy", "slab", None, None, None),
        check_vma=False,
    )
```

```python
import functools

import jax
import jax.numpy as jnp
import ml_dtypes
import numpy as np
from jax import lax
from jax.experimental import pallas as pl
from jax.experimental.pallas import tpu as pltpu
from jax.sharding import PartitionSpec as P

MESH = pl.DeviceIdType.MESH
LANES = 128
PITCH = 16


def split(table):
    high = table.astype(ml_dtypes.bfloat16)
    low = (table - high.astype(np.float64)).astype(ml_dtypes.bfloat16)
    return high, low


def make_tables(count, rows, pitch):
    length = 2 * count
    phases = np.outer(np.arange(count), np.arange(length)) % length
    angles = phases * (2.0 * np.pi / length)
    same = np.zeros((pitch, rows))
    same[np.arange(rows), np.arange(rows)] = 1.0
    high, low = [], []
    for table in (np.cos(angles), np.sin(angles)):
        wide = np.einsum("dk,sr->dsrk", table / length, same).reshape(count * pitch, rows * length)
        for part, into in zip(split(wide), (high, low)):
            into.append(part)
    gather = np.zeros((count * rows, count * pitch), ml_dtypes.bfloat16)
    for owner in range(count):
        for row in range(rows):
            gather[owner * rows + row, owner * pitch + row] = 1.0
    return np.concatenate(high + low, axis=0), gather


def mul(first, second):
    return jnp.dot(first, second, preferred_element_type=jnp.float32)


def mul_t(first, second):
    return lax.dot_general(first, second, (((1,), (1,)), ((), ())), preferred_element_type=jnp.float32)


def sandwich(outer, inner):
    orbitals = outer.shape[1]
    stacked = outer[...].reshape(2 * orbitals, orbitals)
    by_real = mul(stacked, inner[0])
    by_imag = mul(stacked, inner[1])
    half_real = by_real[:orbitals] - by_imag[orbitals:]
    half_imag = by_imag[:orbitals] + by_real[orbitals:]
    half = jnp.concatenate([half_real.astype(jnp.bfloat16), half_imag.astype(jnp.bfloat16)], axis=0)
    with_real = mul_t(half, jnp.concatenate([outer[0], outer[0, LANES:]], axis=0))
    with_imag = mul_t(half, jnp.concatenate([outer[1], outer[1, LANES:]], axis=0))
    full_real = with_real[:orbitals] + with_imag[orbitals:]
    full_imag = with_real[orbitals:] - with_imag[:orbitals]
    low = lax.broadcasted_iota(jnp.int32, (orbitals, LANES), 1) < orbitals - LANES
    return full_real[:, :LANES], full_imag[:, :LANES], jnp.where(low, full_real[:, LANES:], full_imag[:, LANES:])


def kernel(
    n, slabs, rows, pitch,
    green, couple, sigma, screened, inverse,
    recv2,
    outer_v, inner_v, sigma_out, sigma_in, screened_v, inverse_v,
    lines, lags, total, term, send1, recv1, send2,
    local_sem, slab_send, slab_recv, send1_sem, recv1_sem, send2_sem, recv2_sem,
):
    me = lax.axis_index("energy")
    block = lax.axis_index("slab")
    orbitals = outer_v.shape[2]
    length = screened_v.shape[1]
    lag_rows = n * pitch
    tail = orbitals - LANES

    pairs = (
        (green.at[0, 0], outer_v.at[0]), (sigma.at[0, 0], inner_v.at[0]), (couple.at[0, 0], outer_v.at[1]),
        (screened.at[0], screened_v), (inverse, inverse_v),
    )
    loads = [pltpu.make_async_copy(src, dst, local_sem.at[i]) for i, (src, dst) in enumerate(pairs)]
    for load in loads[:2]:
        load.start()

    barrier = pltpu.get_barrier_semaphore()

    def greet(step, _):
        pl.semaphore_signal(barrier, inc=1, device_id=(lax.rem(me + step, n), block), device_id_type=MESH)
        return 0

    @pl.when(block > 0)
    def _():
        pl.semaphore_signal(barrier, inc=1, device_id=(me, block - 1), device_id_type=MESH)

    @pl.when(block < slabs - 1)
    def _():
        pl.semaphore_signal(barrier, inc=1, device_id=(me, block + 1), device_id_type=MESH)

    lax.fori_loop(1, n, greet, 0)

    def everyone_is_here():
        pl.semaphore_wait(barrier, n - 1 + (block > 0).astype(jnp.int32) + (block < slabs - 1).astype(jnp.int32))

    def to_block_before():
        return pltpu.make_async_remote_copy(
            src_ref=sigma_out, dst_ref=sigma_in, send_sem=slab_send, recv_sem=slab_recv,
            device_id=(me, lax.max(block - 1, 0)), device_id_type=MESH,
        )

    term[...] = jnp.zeros_like(term)
    loads[0].wait()
    loads[1].wait()
    for load in loads[2:]:
        load.start()

    @pl.when(block > 0)
    def _():
        tails = [inner_v[0, part, :, LANES:].astype(jnp.float32) for part in range(2)]
        sigma_out[:, :LANES] = inner_v[0, 0, :, :LANES]
        sigma_out[:, LANES:2 * LANES] = inner_v[0, 1, :, :LANES]
        sigma_out[:, 2 * LANES:] = jnp.concatenate(tails, axis=1).astype(jnp.bfloat16)
        everyone_is_here()
        to_block_before().start()

    def add_term(index, _):
        @pl.when(index == 1)
        def _():
            loads[2].wait()
            to_block_before().wait_recv()
            inner_v[1, 0, :, :LANES] = sigma_in[:, :LANES]
            inner_v[1, 1, :, :LANES] = sigma_in[:, LANES:2 * LANES]
            mixed = sigma_in[:, 2 * LANES:]
            inner_v[1, 0, :, LANES:] = mixed[:, :tail]
            inner_v[1, 1, :, LANES:] = mixed[:, tail:]

        for group, value in enumerate(sandwich(outer_v.at[index], inner_v.at[index])):
            term[:orbitals, group * LANES:(group + 1) * LANES] += value
        return 0

    lax.fori_loop(0, 1 + (block < slabs - 1).astype(jnp.int32), add_term, 0)

    @pl.when(block == slabs - 1)
    def _():
        loads[2].wait()

    @pl.when(block == 0)
    def _():
        everyone_is_here()

    for owner in range(n):
        send1[owner * pitch:(owner + 1) * pitch] = term[owner * rows:owner * rows + pitch].astype(jnp.bfloat16)

    def at(ref, index):
        return ref.at[pl.ds(pl.multiple_of(index * pitch, pitch), pitch)]

    def copy(src, dst, send_sem, recv_sem, peer, slot):
        return pltpu.make_async_remote_copy(
            src_ref=at(src, peer), dst_ref=at(dst, slot), send_sem=send_sem.at[peer], recv_sem=recv_sem.at[slot],
            device_id=(peer, block), device_id_type=MESH,
        )

    def each(act):
        def body(step, _):
            act(step)
            return 0

        lax.fori_loop(1, n, body, 0)

    first = (send1, recv1, send1_sem, recv1_sem)
    second = (send2, recv2, send2_sem, recv2_sem)

    def behind(step):
        return lax.rem(me + n - step, n)

    def ahead(step):
        return lax.rem(me + step, n)

    @pl.when(block > 0)
    def _():
        to_block_before().wait_send()

    each(lambda step: copy(*first, ahead(step), me).start())
    own = pltpu.make_async_copy(at(send1, me), at(recv1, me), recv1_sem.at[me])
    own.start()

    loads[3].wait()
    for row in range(rows):
        where = pl.ds(row * length, length)
        for part in range(2):
            line = screened_v[part, :, row * orbitals:(row + 1) * orbitals].astype(jnp.float32)
            last = line[:, LANES:]
            lines[where, part * LANES:(part + 1) * LANES] = line[:, :LANES].astype(jnp.bfloat16)
            lines[where, (part + 2) * LANES:(part + 3) * LANES] = jnp.concatenate([last, last], axis=1).astype(jnp.bfloat16)
    loads[4].wait()
    count = min(n, 8)

    def make_lags(chunk, _):
        def waves(kind):
            high = pl.ds(pl.multiple_of(kind * lag_rows + chunk * count * pitch, count * pitch), count * pitch)
            low = pl.ds(pl.multiple_of((kind + 2) * lag_rows + chunk * count * pitch, count * pitch), count * pitch)
            return mul(inverse_v[high], lines[...]) + mul(inverse_v[low], lines[...])

        cosine, sine = waves(0), waves(1)
        for group in range(0, 4, 2):
            real, imag = (slice(part * LANES, (part + 1) * LANES) for part in (group, group + 1))
            for lag in range(count):
                own = slice(lag * pitch, (lag + 1) * pitch)
                up = n - 1 + chunk * count + lag
                down = n - 1 - chunk * count - lag
                lags[down, :, real] = cosine[own, real] + sine[own, imag]
                lags[down, :, imag] = cosine[own, imag] - sine[own, real]
                lags[up, :, real] = cosine[own, real] - sine[own, imag]
                lags[up, :, imag] = cosine[own, imag] + sine[own, real]
        return 0

    lax.fori_loop(0, n // count, make_lags, 0)

    sign = jnp.where(lax.broadcasted_iota(jnp.int32, (pitch, LANES), 1) < tail, -1.0, 1.0)
    parts = tuple(slice(part * LANES, (part + 1) * LANES) for part in range(4))

    def take(source, buffer):
        rows_of = buffer[pl.ds(pl.multiple_of(source * pitch, pitch), pitch), :].astype(jnp.float32)
        real, imag, mixed = rows_of[:, parts[0]], rows_of[:, parts[1]], rows_of[:, parts[2]]
        return source, real, imag, mixed, pltpu.roll(mixed, tail, 1) * sign

    def terms(taken, energy):
        source, real, imag, mixed, turned = taken
        lag = energy - source + n - 1
        by_real, by_imag, both_real, both_imag = (lags[lag, :, part] for part in parts)
        return real * by_real - imag * by_imag, real * by_imag + imag * by_real, mixed * both_real + turned * both_imag

    def clear(energy, _):
        total[energy] = jnp.zeros((pitch, 3 * LANES), jnp.float32)
        return 0

    lax.fori_loop(0, n, clear, 0)
    own.wait()

    def arrived(step, _):
        source = behind(step)

        @pl.when(step > 0)
        def _():
            copy(*first, source, source).wait_recv()

        taken = take(source, recv1)
        for energy in range(n):
            for part, value in zip(parts, terms(taken, energy)):
                total[energy, :, part] += value
        return 0

    lax.fori_loop(0, n - 1, arrived, 0)
    source = behind(n - 1)
    copy(*first, source, source).wait_recv()
    taken = take(source, recv1)

    def finish(energy):
        where = pl.ds(pl.multiple_of(energy * pitch, pitch), pitch)
        for part, value in zip(parts, terms(taken, energy)):
            send2[where, part] = (total[energy, :, part] + value).astype(jnp.bfloat16)

    def depart(step):
        finish(ahead(step))
        copy(*second, ahead(step), me).start()

    each(depart)
    finish(me)
    keep = pltpu.make_async_copy(at(send2, me), at(recv2, me), recv2_sem.at[me])
    keep.start()
    each(lambda step: copy(*first, ahead(step), me).wait_send())
    each(lambda step: copy(*second, behind(step), behind(step)).wait_recv())
    keep.wait()
    each(lambda step: copy(*second, ahead(step), me).wait_send())


def unpack(gather, packed, out):
    tail = out.shape[-1] - LANES
    result = mul(gather[...], packed[...]).astype(jnp.bfloat16)
    out[0, 0, 0, :, :LANES] = result[:, :LANES]
    out[0, 0, 1, :, :LANES] = result[:, LANES:2 * LANES]
    out[0, 0, 0, :, LANES:] = result[:, 2 * LANES:2 * LANES + tail]
    out[0, 0, 1, :, LANES:] = result[:, 2 * LANES + tail:]


def shards(n, slabs, green_block, coupling, sigma_lesser, screened):
    orbitals = green_block.shape[-1]
    length = screened.shape[2]
    rows = screened.shape[3] // orbitals
    pitch = -(-rows // PITCH) * PITCH
    assert green_block.shape[0] == 1 and length == 2 * n and rows * n == orbitals and orbitals == LANES + LANES // 2
    inverse, gather = make_tables(n, rows, pitch)
    packed = (n * pitch, 2 * orbitals)
    square = (2, orbitals, orbitals)
    bf16 = jnp.bfloat16
    returned = pl.pallas_call(
        functools.partial(kernel, n, slabs, rows, pitch),
        out_shape=pltpu.VMEM(packed, bf16),
        in_specs=[pl.BlockSpec(memory_space=pl.ANY)] * 5,
        out_specs=pl.BlockSpec(memory_space=pltpu.VMEM),
        scratch_shapes=[
            pltpu.VMEM((2, *square), bf16),
            pltpu.VMEM((2, *square), bf16),
            pltpu.VMEM((orbitals, 3 * LANES), bf16),
            pltpu.VMEM((orbitals, 3 * LANES), bf16),
            pltpu.VMEM(screened.shape[1:], bf16),
            pltpu.VMEM(inverse.shape, bf16),
            pltpu.VMEM((rows * length, 4 * LANES), bf16),
            pltpu.VMEM((2 * n - 1, pitch, 4 * LANES), jnp.float32),
            pltpu.VMEM((n, pitch, 3 * LANES), jnp.float32),
            pltpu.VMEM((orbitals + pitch, 3 * LANES), jnp.float32),
            pltpu.VMEM(packed, bf16),
            pltpu.VMEM(packed, bf16),
            pltpu.VMEM(packed, bf16),
            pltpu.SemaphoreType.DMA((5,)),
            pltpu.SemaphoreType.DMA,
            pltpu.SemaphoreType.DMA,
            *[pltpu.SemaphoreType.DMA((n,))] * 4,
        ],
        compiler_params=pltpu.CompilerParams(
            collective_id=0, has_side_effects=True, vmem_limit_bytes=56 * 1024 * 1024
        ),
        cost_estimate=pl.CostEstimate(flops=10**9, bytes_accessed=4 * 10**6, transcendentals=0),
        name="self_energy",
    )(green_block, coupling, sigma_lesser, screened, jnp.asarray(inverse))
    return pl.pallas_call(
        unpack,
        out_shape=jax.ShapeDtypeStruct(green_block.shape, bf16),
        in_specs=[pl.BlockSpec(memory_space=pltpu.VMEM)] * 2,
        out_specs=pl.BlockSpec(memory_space=pltpu.VMEM),
        name="unpack",
    )(jnp.asarray(gather), returned)


def solution(mesh):
    placed = (
        P("energy", "slab", None, None, None),
        P("energy", "slab", None, None, None),
        P("energy", "slab", None, None, None),
        P("slab", None, None, "energy"),
    )
    return jax.shard_map(
        functools.partial(shards, mesh.shape["energy"], mesh.shape["slab"]),
        mesh=mesh,
        in_specs=placed,
        out_specs=P("energy", "slab", None, None, None),
        check_vma=False,
    )
```

```python
import functools

import jax
import jax.numpy as jnp
import ml_dtypes
import numpy as np
from jax import lax
from jax.experimental import pallas as pl
from jax.experimental.pallas import tpu as pltpu
from jax.sharding import PartitionSpec as P

MESH = pl.DeviceIdType.MESH
LANES = 128
PITCH = 16


def split(table):
    high = table.astype(ml_dtypes.bfloat16)
    low = (table - high.astype(np.float64)).astype(ml_dtypes.bfloat16)
    return high, low


def make_tables(count, rows, pitch):
    length = 2 * count
    phases = np.outer(np.arange(count), np.arange(length)) % length
    angles = phases * (2.0 * np.pi / length)
    same = np.zeros((pitch, rows))
    same[np.arange(rows), np.arange(rows)] = 1.0
    high, low = [], []
    for table in (np.cos(angles), np.sin(angles)):
        wide = np.einsum("dk,sr->dsrk", table / length, same).reshape(count * pitch, rows * length)
        for part, into in zip(split(wide), (high, low)):
            into.append(part)
    return np.concatenate(high + low, axis=0)


def mul(first, second):
    return jnp.dot(first, second, preferred_element_type=jnp.float32)


def mul_t(first, second):
    return lax.dot_general(first, second, (((1,), (1,)), ((), ())), preferred_element_type=jnp.float32)


def sandwich(outer, inner, orbitals):
    stacked = jnp.concatenate([outer[0, :orbitals], outer[1, :orbitals]], axis=0)
    by_real = mul(stacked, inner[0])
    by_imag = mul(stacked, inner[1])
    half_real = by_real[:orbitals] - by_imag[orbitals:]
    half_imag = by_imag[:orbitals] + by_real[orbitals:]
    half = jnp.concatenate([half_real.astype(jnp.bfloat16), half_imag.astype(jnp.bfloat16)], axis=0)
    with_real = mul_t(half, outer[0])
    with_imag = mul_t(half, outer[1])
    full_real = with_real[:orbitals] + with_imag[orbitals:]
    full_imag = with_real[orbitals:] - with_imag[:orbitals]
    low = lax.broadcasted_iota(jnp.int32, (orbitals, LANES), 1) < orbitals - LANES
    return full_real[:, :LANES], full_imag[:, :LANES], jnp.where(low, full_real[:, LANES:], full_imag[:, LANES:])


def kernel(
    n, slabs, rows, pitch,
    green, couple, sigma, screened, inverse,
    recv2,
    green_v, sigma_v, couple_v, sigma_out, sigma_in, outer_v, inner_v, screened_v, inverse_v,
    lines, lags, total, term, send1, recv1, send2,
    local_sem, slab_send, slab_recv, send1_sem, recv1_sem, send2_sem, recv2_sem,
):
    me = lax.axis_index("energy")
    block = lax.axis_index("slab")
    orbitals = green_v.shape[1]
    length = screened_v.shape[1]
    lag_rows = n * pitch
    tail = orbitals - LANES

    pairs = (
        (green.at[0, 0], green_v), (sigma.at[0, 0], sigma_v), (couple.at[0, 0], couple_v),
        (screened.at[0], screened_v), (inverse, inverse_v),
    )
    loads = [pltpu.make_async_copy(src, dst, local_sem.at[i]) for i, (src, dst) in enumerate(pairs)]
    for load in loads[:2]:
        load.start()

    barrier = pltpu.get_barrier_semaphore()

    def greet(step, _):
        pl.semaphore_signal(barrier, inc=1, device_id=(lax.rem(me + step, n), block), device_id_type=MESH)
        return 0

    @pl.when(block > 0)
    def _():
        pl.semaphore_signal(barrier, inc=1, device_id=(me, block - 1), device_id_type=MESH)

    @pl.when(block < slabs - 1)
    def _():
        pl.semaphore_signal(barrier, inc=1, device_id=(me, block + 1), device_id_type=MESH)

    lax.fori_loop(1, n, greet, 0)

    def everyone_is_here():
        pl.semaphore_wait(barrier, n - 1 + (block > 0).astype(jnp.int32) + (block < slabs - 1).astype(jnp.int32))

    def to_block_before():
        return pltpu.make_async_remote_copy(
            src_ref=sigma_out, dst_ref=sigma_in, send_sem=slab_send, recv_sem=slab_recv,
            device_id=(me, lax.max(block - 1, 0)), device_id_type=MESH,
        )

    term[...] = jnp.zeros_like(term)
    inner_v[...] = jnp.zeros_like(inner_v)
    outer_v[...] = jnp.zeros_like(outer_v)

    def set_outer(value):
        outer_v[:, :orbitals, :orbitals] = value[...]
        outer_v[:, orbitals:, :orbitals] = value[:, LANES:]

    loads[0].wait()
    loads[1].wait()
    for load in loads[2:]:
        load.start()

    @pl.when(block > 0)
    def _():
        tails = [sigma_v[part, :, LANES:].astype(jnp.float32) for part in range(2)]
        sigma_out[:, :LANES] = sigma_v[0, :, :LANES]
        sigma_out[:, LANES:2 * LANES] = sigma_v[1, :, :LANES]
        sigma_out[:, 2 * LANES:] = jnp.concatenate(tails, axis=1).astype(jnp.bfloat16)
        everyone_is_here()
        to_block_before().start()

    set_outer(green_v)
    inner_v[:, :orbitals, :orbitals] = sigma_v[...]

    def add_term(index, _):
        @pl.when(index == 1)
        def _():
            loads[2].wait()
            set_outer(couple_v)
            to_block_before().wait_recv()
            inner_v[0, :orbitals, :LANES] = sigma_in[:, :LANES]
            inner_v[1, :orbitals, :LANES] = sigma_in[:, LANES:2 * LANES]
            mixed = sigma_in[:, 2 * LANES:]
            inner_v[0, :orbitals, LANES:orbitals] = mixed[:, :tail]
            inner_v[1, :orbitals, LANES:orbitals] = mixed[:, tail:]

        for group, value in enumerate(sandwich(outer_v, inner_v, orbitals)):
            term[:orbitals, group * LANES:(group + 1) * LANES] += value
        return 0

    lax.fori_loop(0, 1 + (block < slabs - 1).astype(jnp.int32), add_term, 0)

    @pl.when(block == slabs - 1)
    def _():
        loads[2].wait()

    @pl.when(block == 0)
    def _():
        everyone_is_here()

    for owner in range(n):
        send1[owner * pitch:(owner + 1) * pitch] = term[owner * rows:owner * rows + pitch].astype(jnp.bfloat16)

    def at(ref, index):
        return ref.at[pl.ds(pl.multiple_of(index * pitch, pitch), pitch)]

    def copy(src, dst, send_sem, recv_sem, peer, slot):
        return pltpu.make_async_remote_copy(
            src_ref=at(src, peer), dst_ref=at(dst, slot), send_sem=send_sem.at[peer], recv_sem=recv_sem.at[slot],
            device_id=(peer, block), device_id_type=MESH,
        )

    def each(act):
        def body(step, _):
            act(step)
            return 0

        lax.fori_loop(1, n, body, 0)

    first = (send1, recv1, send1_sem, recv1_sem)
    second = (send2, recv2, send2_sem, recv2_sem)

    def behind(step):
        return lax.rem(me + n - step, n)

    def ahead(step):
        return lax.rem(me + step, n)

    each(lambda step: copy(*first, ahead(step), me).start())
    own = pltpu.make_async_copy(at(send1, me), at(recv1, me), recv1_sem.at[me])
    own.start()

    loads[3].wait()
    for row in range(rows):
        where = pl.ds(row * length, length)
        for part in range(2):
            line = screened_v[part, :, row * orbitals:(row + 1) * orbitals].astype(jnp.float32)
            last = line[:, LANES:]
            lines[where, part * LANES:(part + 1) * LANES] = line[:, :LANES].astype(jnp.bfloat16)
            lines[where, (part + 2) * LANES:(part + 3) * LANES] = jnp.concatenate([last, last], axis=1).astype(jnp.bfloat16)
    loads[4].wait()
    count = min(n, 8)

    def make_lags(chunk, _):
        def waves(kind):
            high = pl.ds(pl.multiple_of(kind * lag_rows + chunk * count * pitch, count * pitch), count * pitch)
            low = pl.ds(pl.multiple_of((kind + 2) * lag_rows + chunk * count * pitch, count * pitch), count * pitch)
            return mul(inverse_v[high], lines[...]) + mul(inverse_v[low], lines[...])

        cosine, sine = waves(0), waves(1)
        for group in range(0, 4, 2):
            real, imag = (slice(part * LANES, (part + 1) * LANES) for part in (group, group + 1))
            for lag in range(count):
                own = slice(lag * pitch, (lag + 1) * pitch)
                up = n - 1 + chunk * count + lag
                down = n - 1 - chunk * count - lag
                lags[down, :, real] = cosine[own, real] + sine[own, imag]
                lags[down, :, imag] = cosine[own, imag] - sine[own, real]
                lags[up, :, real] = cosine[own, real] - sine[own, imag]
                lags[up, :, imag] = cosine[own, imag] + sine[own, real]
        return 0

    lax.fori_loop(0, n // count, make_lags, 0)

    sign = jnp.where(lax.broadcasted_iota(jnp.int32, (pitch, LANES), 1) < tail, -1.0, 1.0)
    parts = tuple(slice(part * LANES, (part + 1) * LANES) for part in range(4))

    def take(source, buffer):
        rows_of = buffer[pl.ds(pl.multiple_of(source * pitch, pitch), pitch), :].astype(jnp.float32)
        real, imag, mixed = rows_of[:, parts[0]], rows_of[:, parts[1]], rows_of[:, parts[2]]
        return source, real, imag, mixed, pltpu.roll(mixed, tail, 1) * sign

    def terms(taken, energy):
        source, real, imag, mixed, turned = taken
        lag = energy - source + n - 1
        by_real, by_imag, both_real, both_imag = (lags[lag, :, part] for part in parts)
        return real * by_real - imag * by_imag, real * by_imag + imag * by_real, mixed * both_real + turned * both_imag

    def clear(energy, _):
        total[energy] = jnp.zeros((pitch, 3 * LANES), jnp.float32)
        return 0

    lax.fori_loop(0, n, clear, 0)
    own.wait()

    def arrived(step, _):
        source = behind(step)

        @pl.when(step > 0)
        def _():
            copy(*first, source, source).wait_recv()

        taken = take(source, recv1)
        for energy in range(n):
            for part, value in zip(parts, terms(taken, energy)):
                total[energy, :, part] += value
        return 0

    lax.fori_loop(0, n - 1, arrived, 0)
    source = behind(n - 1)
    copy(*first, source, source).wait_recv()
    taken = take(source, recv1)

    def finish(energy):
        where = pl.ds(pl.multiple_of(energy * pitch, pitch), pitch)
        for part, value in zip(parts, terms(taken, energy)):
            send2[where, part] = (total[energy, :, part] + value).astype(jnp.bfloat16)

    def depart(step):
        finish(ahead(step))
        copy(*second, ahead(step), me).start()

    each(depart)
    finish(me)
    keep = pltpu.make_async_copy(at(send2, me), at(recv2, me), recv2_sem.at[me])
    keep.start()
    each(lambda step: copy(*first, ahead(step), me).wait_send())

    @pl.when(block > 0)
    def _():
        to_block_before().wait_send()

    each(lambda step: copy(*second, behind(step), behind(step)).wait_recv())
    keep.wait()
    each(lambda step: copy(*second, ahead(step), me).wait_send())


def unpack(rows, pitch, packed, out):
    orbitals = out.shape[-1]
    tail = orbitals - LANES
    shape = (orbitals, packed.shape[0])
    to_row = lax.broadcasted_iota(jnp.int32, shape, 0)
    from_row = lax.broadcasted_iota(jnp.int32, shape, 1)
    inside = from_row % pitch
    keep = (inside < rows) & (from_row // pitch * rows + inside == to_row)
    gather = jnp.where(keep, 1.0, 0.0).astype(jnp.bfloat16)
    result = mul(gather, packed[...]).astype(jnp.bfloat16)
    out[0, 0, 0, :, :LANES] = result[:, :LANES]
    out[0, 0, 1, :, :LANES] = result[:, LANES:2 * LANES]
    out[0, 0, 0, :, LANES:] = result[:, 2 * LANES:2 * LANES + tail]
    out[0, 0, 1, :, LANES:] = result[:, 2 * LANES + tail:]


def shards(n, slabs, green_block, coupling, sigma_lesser, screened):
    orbitals = green_block.shape[-1]
    length = screened.shape[2]
    rows = screened.shape[3] // orbitals
    pitch = -(-rows // PITCH) * PITCH
    assert green_block.shape[0] == 1 and length == 2 * n and rows * n == orbitals and orbitals == LANES + LANES // 2
    inverse = make_tables(n, rows, pitch)
    packed = (n * pitch, 2 * orbitals)
    square = (2, orbitals, orbitals)
    bf16 = jnp.bfloat16
    returned = pl.pallas_call(
        functools.partial(kernel, n, slabs, rows, pitch),
        out_shape=pltpu.VMEM(packed, bf16),
        in_specs=[pl.BlockSpec(memory_space=pl.ANY)] * 5,
        out_specs=pl.BlockSpec(memory_space=pltpu.VMEM),
        scratch_shapes=[
            pltpu.VMEM(square, bf16),
            pltpu.VMEM(square, bf16),
            pltpu.VMEM(square, bf16),
            pltpu.VMEM((orbitals, 3 * LANES), bf16),
            pltpu.VMEM((orbitals, 3 * LANES), bf16),
            pltpu.VMEM((2, 2 * LANES, 2 * LANES), bf16),
            pltpu.VMEM((2, 2 * LANES, 2 * LANES), bf16),
            pltpu.VMEM(screened.shape[1:], bf16),
            pltpu.VMEM(inverse.shape, bf16),
            pltpu.VMEM((rows * length, 4 * LANES), bf16),
            pltpu.VMEM((2 * n - 1, pitch, 4 * LANES), jnp.float32),
            pltpu.VMEM((n, pitch, 3 * LANES), jnp.float32),
            pltpu.VMEM((orbitals + pitch, 3 * LANES), jnp.float32),
            pltpu.VMEM(packed, bf16),
            pltpu.VMEM(packed, bf16),
            pltpu.VMEM(packed, bf16),
            pltpu.SemaphoreType.DMA((5,)),
            pltpu.SemaphoreType.DMA,
            pltpu.SemaphoreType.DMA,
            *[pltpu.SemaphoreType.DMA((n,))] * 4,
        ],
        compiler_params=pltpu.CompilerParams(
            collective_id=0, has_side_effects=True, vmem_limit_bytes=56 * 1024 * 1024
        ),
        cost_estimate=pl.CostEstimate(flops=10**9, bytes_accessed=4 * 10**6, transcendentals=0),
        name="self_energy",
    )(green_block, coupling, sigma_lesser, screened, jnp.asarray(inverse))
    return pl.pallas_call(
        functools.partial(unpack, rows, pitch),
        out_shape=jax.ShapeDtypeStruct(green_block.shape, bf16),
        in_specs=[pl.BlockSpec(memory_space=pltpu.VMEM)],
        out_specs=pl.BlockSpec(memory_space=pltpu.VMEM),
        name="unpack",
    )(returned)


def solution(mesh):
    placed = (
        P("energy", "slab", None, None, None),
        P("energy", "slab", None, None, None),
        P("energy", "slab", None, None, None),
        P("slab", None, None, "energy"),
    )
    return jax.shard_map(
        functools.partial(shards, mesh.shape["energy"], mesh.shape["slab"]),
        mesh=mesh,
        in_specs=placed,
        out_specs=P("energy", "slab", None, None, None),
        check_vma=False,
    )
```

```python
import functools

import jax
import jax.numpy as jnp
import ml_dtypes
import numpy as np
from jax import lax
from jax.experimental import pallas as pl
from jax.experimental.pallas import tpu as pltpu
from jax.sharding import PartitionSpec as P

MESH = pl.DeviceIdType.MESH
LANES = 128
PITCH = 16


def split(table):
    high = table.astype(ml_dtypes.bfloat16)
    low = (table - high.astype(np.float64)).astype(ml_dtypes.bfloat16)
    return high, low


def make_tables(count, rows, pitch):
    length = 2 * count
    phases = np.outer(np.arange(count), np.arange(length)) % length
    angles = phases * (2.0 * np.pi / length)
    same = np.zeros((pitch, rows))
    same[np.arange(rows), np.arange(rows)] = 1.0
    high, low = [], []
    for table in (np.cos(angles), np.sin(angles)):
        wide = np.einsum("dk,sr->dsrk", table / length, same).reshape(count * pitch, rows * length)
        for part, into in zip(split(wide), (high, low)):
            into.append(part)
    gather = np.zeros((count * rows, count * pitch), ml_dtypes.bfloat16)
    for owner in range(count):
        for row in range(rows):
            gather[owner * rows + row, owner * pitch + row] = 1.0
    return np.concatenate(high + low, axis=0), gather


def mul(first, second):
    return jnp.dot(first, second, preferred_element_type=jnp.float32)


def mul_t(first, second):
    return lax.dot_general(first, second, (((1,), (1,)), ((), ())), preferred_element_type=jnp.float32)


def sandwich(outer, inner):
    orbitals = outer.shape[1]
    stacked = outer[...].reshape(2 * orbitals, orbitals)
    by_real = mul(stacked, inner[0])
    by_imag = mul(stacked, inner[1])
    half_real = by_real[:orbitals] - by_imag[orbitals:]
    half_imag = by_imag[:orbitals] + by_real[orbitals:]
    half = jnp.concatenate([half_real.astype(jnp.bfloat16), half_imag.astype(jnp.bfloat16)], axis=0)
    with_real = mul_t(half, jnp.concatenate([outer[0], outer[0, LANES:]], axis=0))
    with_imag = mul_t(half, jnp.concatenate([outer[1], outer[1, LANES:]], axis=0))
    full_real = with_real[:orbitals] + with_imag[orbitals:]
    full_imag = with_real[orbitals:] - with_imag[:orbitals]
    low = lax.broadcasted_iota(jnp.int32, (orbitals, LANES), 1) < orbitals - LANES
    return full_real[:, :LANES], full_imag[:, :LANES], jnp.where(low, full_real[:, LANES:], full_imag[:, LANES:])


def kernel(
    n, slabs, rows, pitch,
    green, couple, sigma, screened, inverse,
    recv2,
    outer_v, inner_v, screened_v, inverse_v,
    lines, lags, total, term, send1, recv1, send2,
    local_sem, slab_send, slab_recv, send1_sem, recv1_sem, send2_sem, recv2_sem,
):
    me = lax.axis_index("energy")
    block = lax.axis_index("slab")
    orbitals = outer_v.shape[2]
    length = screened_v.shape[1]
    lag_rows = n * pitch
    tail = orbitals - LANES

    pairs = (
        (green.at[0, 0], outer_v.at[0]), (sigma.at[0, 0], inner_v.at[0]), (couple.at[0, 0], outer_v.at[1]),
        (screened.at[0], screened_v), (inverse, inverse_v),
    )
    loads = [pltpu.make_async_copy(src, dst, local_sem.at[i]) for i, (src, dst) in enumerate(pairs)]
    for load in loads[:2]:
        load.start()

    barrier = pltpu.get_barrier_semaphore()

    def greet(step, _):
        pl.semaphore_signal(barrier, inc=1, device_id=(lax.rem(me + step, n), block), device_id_type=MESH)
        return 0

    @pl.when(block > 0)
    def _():
        pl.semaphore_signal(barrier, inc=1, device_id=(me, block - 1), device_id_type=MESH)

    @pl.when(block < slabs - 1)
    def _():
        pl.semaphore_signal(barrier, inc=1, device_id=(me, block + 1), device_id_type=MESH)

    lax.fori_loop(1, n, greet, 0)

    def everyone_is_here():
        pl.semaphore_wait(barrier, n - 1 + (block > 0).astype(jnp.int32) + (block < slabs - 1).astype(jnp.int32))

    def to_block_before():
        return pltpu.make_async_remote_copy(
            src_ref=sigma.at[0, 0], dst_ref=inner_v.at[1], send_sem=slab_send, recv_sem=slab_recv,
            device_id=(me, lax.max(block - 1, 0)), device_id_type=MESH,
        )

    term[...] = jnp.zeros_like(term)
    loads[0].wait()
    loads[1].wait()
    for load in loads[2:]:
        load.start()

    @pl.when(block > 0)
    def _():
        everyone_is_here()
        to_block_before().start()

    def add_term(index, _):
        @pl.when(index == 1)
        def _():
            loads[2].wait()
            to_block_before().wait_recv()

        for group, value in enumerate(sandwich(outer_v.at[index], inner_v.at[index])):
            term[:orbitals, group * LANES:(group + 1) * LANES] += value
        return 0

    lax.fori_loop(0, 1 + (block < slabs - 1).astype(jnp.int32), add_term, 0)

    @pl.when(block == slabs - 1)
    def _():
        loads[2].wait()

    @pl.when(block == 0)
    def _():
        everyone_is_here()

    for owner in range(n):
        send1[owner * pitch:(owner + 1) * pitch] = term[owner * rows:owner * rows + pitch].astype(jnp.bfloat16)

    def at(ref, index):
        return ref.at[pl.ds(pl.multiple_of(index * pitch, pitch), pitch)]

    def copy(src, dst, send_sem, recv_sem, peer, slot):
        return pltpu.make_async_remote_copy(
            src_ref=at(src, peer), dst_ref=at(dst, slot), send_sem=send_sem.at[peer], recv_sem=recv_sem.at[slot],
            device_id=(peer, block), device_id_type=MESH,
        )

    def distance(turn):
        return n // 2 + (turn + 1) // 2 * ((turn + 1) % 2 * 2 - 1)

    def each(act):
        def body(turn, _):
            act(distance(turn))
            return 0

        lax.fori_loop(0, n - 1, body, 0, unroll=n <= 16)

    first = (send1, recv1, send1_sem, recv1_sem)
    second = (send2, recv2, send2_sem, recv2_sem)

    def behind(step):
        return lax.rem(me + n - step, n)

    def ahead(step):
        return lax.rem(me + step, n)

    each(lambda step: copy(*first, ahead(step), me).start())
    own = pltpu.make_async_copy(at(send1, me), at(recv1, me), recv1_sem.at[me])
    own.start()

    loads[3].wait()
    for row in range(rows):
        where = pl.ds(row * length, length)
        for part in range(2):
            line = screened_v[part, :, row * orbitals:(row + 1) * orbitals].astype(jnp.float32)
            last = line[:, LANES:]
            lines[where, part * LANES:(part + 1) * LANES] = line[:, :LANES].astype(jnp.bfloat16)
            lines[where, (part + 2) * LANES:(part + 3) * LANES] = jnp.concatenate([last, last], axis=1).astype(jnp.bfloat16)
    loads[4].wait()
    count = min(n, 8)

    def make_lags(chunk, _):
        def waves(kind):
            high = pl.ds(pl.multiple_of(kind * lag_rows + chunk * count * pitch, count * pitch), count * pitch)
            low = pl.ds(pl.multiple_of((kind + 2) * lag_rows + chunk * count * pitch, count * pitch), count * pitch)
            return mul(inverse_v[high], lines[...]) + mul(inverse_v[low], lines[...])

        cosine, sine = waves(0), waves(1)
        for group in range(0, 4, 2):
            real, imag = (slice(part * LANES, (part + 1) * LANES) for part in (group, group + 1))
            for lag in range(count):
                own = slice(lag * pitch, (lag + 1) * pitch)
                up = n - 1 + chunk * count + lag
                down = n - 1 - chunk * count - lag
                lags[down, :, real] = cosine[own, real] + sine[own, imag]
                lags[down, :, imag] = cosine[own, imag] - sine[own, real]
                lags[up, :, real] = cosine[own, real] - sine[own, imag]
                lags[up, :, imag] = cosine[own, imag] + sine[own, real]
        return 0

    lax.fori_loop(0, n // count, make_lags, 0)

    sign = jnp.where(lax.broadcasted_iota(jnp.int32, (pitch, LANES), 1) < tail, -1.0, 1.0)
    parts = tuple(slice(part * LANES, (part + 1) * LANES) for part in range(4))

    def take(source, buffer):
        rows_of = buffer[pl.ds(pl.multiple_of(source * pitch, pitch), pitch), :].astype(jnp.float32)
        real, imag, mixed = rows_of[:, parts[0]], rows_of[:, parts[1]], rows_of[:, parts[2]]
        return source, real, imag, mixed, pltpu.roll(mixed, tail, 1) * sign

    def terms(taken, energy):
        source, real, imag, mixed, turned = taken
        lag = energy - source + n - 1
        by_real, by_imag, both_real, both_imag = (lags[lag, :, part] for part in parts)
        return real * by_real - imag * by_imag, real * by_imag + imag * by_real, mixed * both_real + turned * both_imag

    own.wait()

    def both(turn):
        taken = []
        for source in (behind(distance(turn)), behind(distance(turn + 1))):
            copy(*first, source, source).wait_recv()
            taken.append(take(source, recv1))
        return taken

    def add(taken, energy):
        return [one + other for one, other in zip(terms(taken[0], energy), terms(taken[1], energy))]

    mine = take(me, recv1)
    source = behind(distance(0))
    copy(*first, source, source).wait_recv()
    taken = [mine, take(source, recv1)]

    def begin(energy, _):
        for part, value in zip(parts, add(taken, energy)):
            total[energy, :, part] = value
        return 0

    lax.fori_loop(0, n, begin, 0, unroll=n <= 16)

    def arrived(pair, _):
        taken = both(2 * pair + 1)
        for energy in range(n):
            for part, value in zip(parts, add(taken, energy)):
                total[energy, :, part] += value
        return 0

    lax.fori_loop(0, n // 2 - 2, arrived, 0)
    taken = both(n - 3)

    def finish(energy):
        where = pl.ds(pl.multiple_of(energy * pitch, pitch), pitch)
        for part, value in zip(parts, add(taken, energy)):
            send2[where, part] = (total[energy, :, part] + value).astype(jnp.bfloat16)

    def depart(step):
        finish(ahead(step))
        copy(*second, ahead(step), me).start()

    each(depart)
    finish(me)
    keep = pltpu.make_async_copy(at(send2, me), at(recv2, me), recv2_sem.at[me])
    keep.start()
    each(lambda step: copy(*first, ahead(step), me).wait_send())

    @pl.when(block > 0)
    def _():
        to_block_before().wait_send()

    each(lambda step: copy(*second, behind(step), behind(step)).wait_recv())
    keep.wait()
    each(lambda step: copy(*second, ahead(step), me).wait_send())


def unpack(gather, packed, out):
    tail = out.shape[-1] - LANES
    result = mul(gather[...], packed[...]).astype(jnp.bfloat16)
    out[0, 0, 0, :, :LANES] = result[:, :LANES]
    out[0, 0, 1, :, :LANES] = result[:, LANES:2 * LANES]
    out[0, 0, 0, :, LANES:] = result[:, 2 * LANES:2 * LANES + tail]
    out[0, 0, 1, :, LANES:] = result[:, 2 * LANES + tail:]


def shards(n, slabs, green_block, coupling, sigma_lesser, screened):
    orbitals = green_block.shape[-1]
    length = screened.shape[2]
    rows = screened.shape[3] // orbitals
    pitch = -(-rows // PITCH) * PITCH
    assert green_block.shape[0] == 1 and length == 2 * n and rows * n == orbitals and orbitals == LANES + LANES // 2
    inverse, gather = make_tables(n, rows, pitch)
    packed = (n * pitch, 2 * orbitals)
    square = (2, orbitals, orbitals)
    bf16 = jnp.bfloat16
    returned = pl.pallas_call(
        functools.partial(kernel, n, slabs, rows, pitch),
        out_shape=pltpu.VMEM(packed, bf16),
        in_specs=[pl.BlockSpec(memory_space=pl.ANY)] * 5,
        out_specs=pl.BlockSpec(memory_space=pltpu.VMEM),
        scratch_shapes=[
            pltpu.VMEM((2, *square), bf16),
            pltpu.VMEM((2, *square), bf16),
            pltpu.VMEM(screened.shape[1:], bf16),
            pltpu.VMEM(inverse.shape, bf16),
            pltpu.VMEM((rows * length, 4 * LANES), bf16),
            pltpu.VMEM((2 * n - 1, pitch, 4 * LANES), jnp.float32),
            pltpu.VMEM((n, pitch, 3 * LANES), jnp.float32),
            pltpu.VMEM((orbitals + pitch, 3 * LANES), jnp.float32),
            pltpu.VMEM(packed, bf16),
            pltpu.VMEM(packed, bf16),
            pltpu.VMEM(packed, bf16),
            pltpu.SemaphoreType.DMA((5,)),
            pltpu.SemaphoreType.DMA,
            pltpu.SemaphoreType.DMA,
            *[pltpu.SemaphoreType.DMA((n,))] * 4,
        ],
        compiler_params=pltpu.CompilerParams(
            collective_id=0, has_side_effects=True, vmem_limit_bytes=56 * 1024 * 1024
        ),
        cost_estimate=pl.CostEstimate(flops=10**9, bytes_accessed=4 * 10**6, transcendentals=0),
        name="self_energy",
    )(green_block, coupling, sigma_lesser, screened, jnp.asarray(inverse))
    return pl.pallas_call(
        unpack,
        out_shape=jax.ShapeDtypeStruct(green_block.shape, bf16),
        in_specs=[pl.BlockSpec(memory_space=pltpu.VMEM)] * 2,
        out_specs=pl.BlockSpec(memory_space=pltpu.VMEM),
        name="unpack",
    )(jnp.asarray(gather), pltpu.with_memory_space_constraint(returned, pltpu.VMEM))


def solution(mesh):
    placed = (
        P("energy", "slab", None, None, None),
        P("energy", "slab", None, None, None),
        P("energy", "slab", None, None, None),
        P("slab", None, None, "energy"),
    )
    return jax.shard_map(
        functools.partial(shards, mesh.shape["energy"], mesh.shape["slab"]),
        mesh=mesh,
        in_specs=placed,
        out_specs=P("energy", "slab", None, None, None),
        check_vma=False,
    )
```

```python
import functools

import jax
import jax.numpy as jnp
import ml_dtypes
import numpy as np
from jax import lax
from jax.experimental import pallas as pl
from jax.experimental.pallas import tpu as pltpu
from jax.sharding import PartitionSpec as P

MESH = pl.DeviceIdType.MESH
LANES = 128
PITCH = 16


def split(table):
    high = table.astype(ml_dtypes.bfloat16)
    low = (table - high.astype(np.float64)).astype(ml_dtypes.bfloat16)
    return high, low


def make_tables(count, rows, pitch):
    length = 2 * count
    phases = np.outer(np.arange(count), np.arange(length)) % length
    angles = phases * (2.0 * np.pi / length)
    same = np.zeros((pitch, rows))
    same[np.arange(rows), np.arange(rows)] = 1.0
    high, low = [], []
    for table in (np.cos(angles), np.sin(angles)):
        wide = np.einsum("dk,sr->dsrk", table / length, same).reshape(count * pitch, rows * length)
        for part, into in zip(split(wide), (high, low)):
            into.append(part)
    return np.concatenate(high + low, axis=0)


def mul(first, second):
    return jnp.dot(first, second, preferred_element_type=jnp.float32)


def mul_t(first, second):
    return lax.dot_general(first, second, (((1,), (1,)), ((), ())), preferred_element_type=jnp.float32)


def sandwich(outer, inner):
    orbitals = outer.shape[1]
    stacked = outer[...].reshape(2 * orbitals, orbitals)
    by_real = mul(stacked, inner[0])
    by_imag = mul(stacked, inner[1])
    half_real = by_real[:orbitals] - by_imag[orbitals:]
    half_imag = by_imag[:orbitals] + by_real[orbitals:]
    half = jnp.concatenate([half_real.astype(jnp.bfloat16), half_imag.astype(jnp.bfloat16)], axis=0)
    with_real = mul_t(half, jnp.concatenate([outer[0], outer[0, LANES:]], axis=0))
    with_imag = mul_t(half, jnp.concatenate([outer[1], outer[1, LANES:]], axis=0))
    full_real = with_real[:orbitals] + with_imag[orbitals:]
    full_imag = with_real[orbitals:] - with_imag[:orbitals]
    low = lax.broadcasted_iota(jnp.int32, (orbitals, LANES), 1) < orbitals - LANES
    return full_real[:, :LANES], full_imag[:, :LANES], jnp.where(low, full_real[:, LANES:], full_imag[:, LANES:])


def kernel(
    n, slabs, rows, pitch,
    green, couple, sigma, screened, inverse,
    recv2,
    outer_v, inner_v, screened_v, inverse_v,
    lines, lags, total, term, send1, recv1, send2,
    local_sem, slab_send, slab_recv, send1_sem, recv1_sem, send2_sem, recv2_sem,
):
    me = lax.axis_index("energy")
    block = lax.axis_index("slab")
    orbitals = outer_v.shape[2]
    length = screened_v.shape[1]
    lag_rows = n * pitch
    tail = orbitals - LANES

    pairs = (
        (green.at[0, 0], outer_v.at[0]), (sigma.at[0, 0], inner_v.at[0]), (couple.at[0, 0], outer_v.at[1]),
        (screened.at[0], screened_v), (inverse, inverse_v),
    )
    loads = [pltpu.make_async_copy(src, dst, local_sem.at[i]) for i, (src, dst) in enumerate(pairs)]
    for load in loads[:2]:
        load.start()

    barrier = pltpu.get_barrier_semaphore()

    def greet(step, _):
        pl.semaphore_signal(barrier, inc=1, device_id=(lax.rem(me + step, n), block), device_id_type=MESH)
        return 0

    @pl.when(block > 0)
    def _():
        pl.semaphore_signal(barrier, inc=1, device_id=(me, block - 1), device_id_type=MESH)

    @pl.when(block < slabs - 1)
    def _():
        pl.semaphore_signal(barrier, inc=1, device_id=(me, block + 1), device_id_type=MESH)

    lax.fori_loop(1, n, greet, 0)

    def everyone_is_here():
        pl.semaphore_wait(barrier, n - 1 + (block > 0).astype(jnp.int32) + (block < slabs - 1).astype(jnp.int32))

    def to_block_before():
        return pltpu.make_async_remote_copy(
            src_ref=sigma.at[0, 0], dst_ref=inner_v.at[1], send_sem=slab_send, recv_sem=slab_recv,
            device_id=(me, lax.max(block - 1, 0)), device_id_type=MESH,
        )

    term[...] = jnp.zeros_like(term)
    loads[0].wait()
    loads[1].wait()
    for load in loads[2:]:
        load.start()

    @pl.when(block > 0)
    def _():
        everyone_is_here()
        to_block_before().start()

    def add_term(index, _):
        @pl.when(index == 1)
        def _():
            loads[2].wait()
            to_block_before().wait_recv()

        for group, value in enumerate(sandwich(outer_v.at[index], inner_v.at[index])):
            term[:orbitals, group * LANES:(group + 1) * LANES] += value
        return 0

    lax.fori_loop(0, 1 + (block < slabs - 1).astype(jnp.int32), add_term, 0)

    @pl.when(block == slabs - 1)
    def _():
        loads[2].wait()

    @pl.when(block == 0)
    def _():
        everyone_is_here()

    for owner in range(n):
        send1[owner * pitch:(owner + 1) * pitch] = term[owner * rows:owner * rows + pitch].astype(jnp.bfloat16)

    def at(ref, index):
        return ref.at[pl.ds(pl.multiple_of(index * pitch, pitch), pitch)]

    def copy(src, dst, send_sem, recv_sem, peer, slot):
        return pltpu.make_async_remote_copy(
            src_ref=at(src, peer), dst_ref=at(dst, slot), send_sem=send_sem.at[peer], recv_sem=recv_sem.at[slot],
            device_id=(peer, block), device_id_type=MESH,
        )

    def distance(turn):
        return turn + 1

    def each(act):
        def body(turn, _):
            act(distance(turn))
            return 0

        lax.fori_loop(0, n - 1, body, 0, unroll=n <= 16)

    first = (send1, recv1, send1_sem, recv1_sem)
    second = (send2, recv2, send2_sem, recv2_sem)

    def behind(step):
        return lax.rem(me + n - step, n)

    def ahead(step):
        return lax.rem(me + step, n)

    each(lambda step: copy(*first, ahead(step), me).start())
    own = pltpu.make_async_copy(at(send1, me), at(recv1, me), recv1_sem.at[me])
    own.start()

    loads[3].wait()
    for row in range(rows):
        where = pl.ds(row * length, length)
        for part in range(2):
            line = screened_v[part, :, row * orbitals:(row + 1) * orbitals].astype(jnp.float32)
            last = line[:, LANES:]
            lines[where, part * LANES:(part + 1) * LANES] = line[:, :LANES].astype(jnp.bfloat16)
            lines[where, (part + 2) * LANES:(part + 3) * LANES] = jnp.concatenate([last, last], axis=1).astype(jnp.bfloat16)
    loads[4].wait()
    count = min(n, 8)

    def make_lags(chunk, _):
        def waves(kind):
            high = pl.ds(pl.multiple_of(kind * lag_rows + chunk * count * pitch, count * pitch), count * pitch)
            low = pl.ds(pl.multiple_of((kind + 2) * lag_rows + chunk * count * pitch, count * pitch), count * pitch)
            return mul(inverse_v[high], lines[...]) + mul(inverse_v[low], lines[...])

        cosine, sine = waves(0), waves(1)
        for group in range(0, 4, 2):
            real, imag = (slice(part * LANES, (part + 1) * LANES) for part in (group, group + 1))
            for lag in range(count):
                own = slice(lag * pitch, (lag + 1) * pitch)
                up = n - 1 + chunk * count + lag
                down = n - 1 - chunk * count - lag
                lags[down, :, real] = cosine[own, real] + sine[own, imag]
                lags[down, :, imag] = cosine[own, imag] - sine[own, real]
                lags[up, :, real] = cosine[own, real] - sine[own, imag]
                lags[up, :, imag] = cosine[own, imag] + sine[own, real]
        return 0

    lax.fori_loop(0, n // count, make_lags, 0)

    sign = jnp.where(lax.broadcasted_iota(jnp.int32, (pitch, LANES), 1) < tail, -1.0, 1.0)
    parts = tuple(slice(part * LANES, (part + 1) * LANES) for part in range(4))

    def take(source, buffer):
        rows_of = buffer[pl.ds(pl.multiple_of(source * pitch, pitch), pitch), :].astype(jnp.float32)
        real, imag, mixed = rows_of[:, parts[0]], rows_of[:, parts[1]], rows_of[:, parts[2]]
        return source, real, imag, mixed, pltpu.roll(mixed, tail, 1) * sign

    def terms(taken, energy):
        source, real, imag, mixed, turned = taken
        lag = energy - source + n - 1
        by_real, by_imag, both_real, both_imag = (lags[lag, :, part] for part in parts)
        return real * by_real - imag * by_imag, real * by_imag + imag * by_real, mixed * both_real + turned * both_imag

    own.wait()

    def both(turn):
        taken = []
        for source in (behind(distance(turn)), behind(distance(turn + 1))):
            copy(*first, source, source).wait_recv()
            taken.append(take(source, recv1))
        return taken

    def add(taken, energy):
        return [one + other for one, other in zip(terms(taken[0], energy), terms(taken[1], energy))]

    mine = take(me, recv1)
    source = behind(distance(0))
    copy(*first, source, source).wait_recv()
    taken = [mine, take(source, recv1)]

    def begin(energy, _):
        for part, value in zip(parts, add(taken, energy)):
            total[energy, :, part] = value
        return 0

    lax.fori_loop(0, n, begin, 0, unroll=n <= 16)

    def arrived(pair, _):
        taken = both(2 * pair + 1)
        for energy in range(n):
            for part, value in zip(parts, add(taken, energy)):
                total[energy, :, part] += value
        return 0

    lax.fori_loop(0, n // 2 - 2, arrived, 0)
    taken = both(n - 3)

    def finish(energy):
        where = pl.ds(pl.multiple_of(energy * pitch, pitch), pitch)
        for part, value in zip(parts, add(taken, energy)):
            send2[where, part] = (total[energy, :, part] + value).astype(jnp.bfloat16)

    def depart(step):
        finish(ahead(step))
        copy(*second, ahead(step), me).start()

    each(depart)
    finish(me)
    keep = pltpu.make_async_copy(at(send2, me), at(recv2, me), recv2_sem.at[me])
    keep.start()
    each(lambda step: copy(*first, ahead(step), me).wait_send())

    @pl.when(block > 0)
    def _():
        to_block_before().wait_send()

    each(lambda step: copy(*second, behind(step), behind(step)).wait_recv())
    keep.wait()
    each(lambda step: copy(*second, ahead(step), me).wait_send())


def unpack(rows, pitch, packed, out, spread):
    orbitals = out.shape[-1]
    tail = orbitals - LANES
    for owner in range(orbitals // rows):
        block = packed[owner * pitch:(owner + 1) * pitch].astype(jnp.float32)
        spread[owner * rows:owner * rows + pitch] = block
    result = spread[:orbitals].astype(jnp.bfloat16)
    out[0, 0, 0, :, :LANES] = result[:, :LANES]
    out[0, 0, 1, :, :LANES] = result[:, LANES:2 * LANES]
    out[0, 0, 0, :, LANES:] = result[:, 2 * LANES:2 * LANES + tail]
    out[0, 0, 1, :, LANES:] = result[:, 2 * LANES + tail:]


def shards(n, slabs, green_block, coupling, sigma_lesser, screened):
    orbitals = green_block.shape[-1]
    length = screened.shape[2]
    rows = screened.shape[3] // orbitals
    pitch = -(-rows // PITCH) * PITCH
    assert green_block.shape[0] == 1 and length == 2 * n and rows * n == orbitals and orbitals == LANES + LANES // 2
    inverse = make_tables(n, rows, pitch)
    packed = (n * pitch, 2 * orbitals)
    square = (2, orbitals, orbitals)
    bf16 = jnp.bfloat16
    returned = pl.pallas_call(
        functools.partial(kernel, n, slabs, rows, pitch),
        out_shape=pltpu.VMEM(packed, bf16),
        in_specs=[pl.BlockSpec(memory_space=pl.ANY)] * 5,
        out_specs=pl.BlockSpec(memory_space=pltpu.VMEM),
        scratch_shapes=[
            pltpu.VMEM((2, *square), bf16),
            pltpu.VMEM((2, *square), bf16),
            pltpu.VMEM(screened.shape[1:], bf16),
            pltpu.VMEM(inverse.shape, bf16),
            pltpu.VMEM((rows * length, 4 * LANES), bf16),
            pltpu.VMEM((2 * n - 1, pitch, 4 * LANES), jnp.float32),
            pltpu.VMEM((n, pitch, 3 * LANES), jnp.float32),
            pltpu.VMEM((orbitals + pitch, 3 * LANES), jnp.float32),
            pltpu.VMEM(packed, bf16),
            pltpu.VMEM(packed, bf16),
            pltpu.VMEM(packed, bf16),
            pltpu.SemaphoreType.DMA((5,)),
            pltpu.SemaphoreType.DMA,
            pltpu.SemaphoreType.DMA,
            *[pltpu.SemaphoreType.DMA((n,))] * 4,
        ],
        compiler_params=pltpu.CompilerParams(
            collective_id=0, has_side_effects=True, vmem_limit_bytes=56 * 1024 * 1024
        ),
        cost_estimate=pl.CostEstimate(flops=10**9, bytes_accessed=4 * 10**6, transcendentals=0),
        name="self_energy",
    )(green_block, coupling, sigma_lesser, screened, jnp.asarray(inverse))
    return pl.pallas_call(
        functools.partial(unpack, rows, pitch),
        out_shape=jax.ShapeDtypeStruct(green_block.shape, bf16),
        in_specs=[pl.BlockSpec(memory_space=pltpu.VMEM)],
        out_specs=pl.BlockSpec(memory_space=pltpu.VMEM),
        scratch_shapes=[pltpu.VMEM((orbitals + pitch, 3 * LANES), jnp.float32)],
        name="unpack",
    )(pltpu.with_memory_space_constraint(returned, pltpu.VMEM))


def solution(mesh):
    placed = (
        P("energy", "slab", None, None, None),
        P("energy", "slab", None, None, None),
        P("energy", "slab", None, None, None),
        P("slab", None, None, "energy"),
    )
    return jax.shard_map(
        functools.partial(shards, mesh.shape["energy"], mesh.shape["slab"]),
        mesh=mesh,
        in_specs=placed,
        out_specs=P("energy", "slab", None, None, None),
        check_vma=False,
    )
```

```python
import functools

import jax
import jax.numpy as jnp
import ml_dtypes
import numpy as np
from jax import lax
from jax.experimental import pallas as pl
from jax.experimental.pallas import tpu as pltpu
from jax.sharding import PartitionSpec as P

MESH = pl.DeviceIdType.MESH
LANES = 128
PITCH = 16


def split(table):
    high = table.astype(ml_dtypes.bfloat16)
    low = (table - high.astype(np.float64)).astype(ml_dtypes.bfloat16)
    return high, low


def make_tables(count, rows, pitch):
    length = 2 * count
    phases = np.outer(np.arange(count), np.arange(length)) % length
    angles = phases * (2.0 * np.pi / length)
    same = np.zeros((pitch, rows))
    same[np.arange(rows), np.arange(rows)] = 1.0
    high, low = [], []
    for table in (np.cos(angles), np.sin(angles)):
        wide = np.einsum("dk,sr->dsrk", table / length, same).reshape(count * pitch, rows * length)
        for part, into in zip(split(wide), (high, low)):
            into.append(part)
    return np.concatenate(high + low, axis=0)


def mul(first, second):
    return jnp.dot(first, second, preferred_element_type=jnp.float32)


def mul_t(first, second):
    return lax.dot_general(first, second, (((1,), (1,)), ((), ())), preferred_element_type=jnp.float32)


def sandwich(outer, inner):
    orbitals = outer.shape[1]
    stacked = outer[...].reshape(2 * orbitals, orbitals)
    both = mul(stacked, inner[...])
    by_real, by_imag = both[:, :orbitals], both[:, 2 * LANES:2 * LANES + orbitals]
    half_real = by_real[:orbitals] - by_imag[orbitals:]
    half_imag = by_imag[:orbitals] + by_real[orbitals:]
    half = jnp.concatenate([half_real.astype(jnp.bfloat16), half_imag.astype(jnp.bfloat16)], axis=0)
    right = jnp.concatenate([outer[0], outer[0, LANES:], outer[1], outer[1, LANES:]], axis=0)
    both = mul_t(half, right)
    with_real, with_imag = both[:, :2 * LANES], both[:, 2 * LANES:]
    full_real = with_real[:orbitals] + with_imag[orbitals:]
    full_imag = with_real[orbitals:] - with_imag[:orbitals]
    low = lax.broadcasted_iota(jnp.int32, (orbitals, LANES), 1) < orbitals - LANES
    return full_real[:, :LANES], full_imag[:, :LANES], jnp.where(low, full_real[:, LANES:], full_imag[:, LANES:])


def kernel(
    n, slabs, rows, pitch,
    green, couple, sigma, screened, inverse,
    recv2,
    outer_v, sigma_v, inner_v, screened_v, inverse_v,
    lines, lags, total, term, send1, recv1, send2,
    local_sem, slab_send, slab_recv, send1_sem, recv1_sem, send2_sem, recv2_sem,
):
    me = lax.axis_index("energy")
    block = lax.axis_index("slab")
    orbitals = outer_v.shape[2]
    length = screened_v.shape[1]
    lag_rows = n * pitch
    tail = orbitals - LANES

    pairs = (
        (green.at[0, 0], outer_v.at[0]), (sigma.at[0, 0], sigma_v.at[0]), (couple.at[0, 0], outer_v.at[1]),
        (screened.at[0], screened_v), (inverse, inverse_v),
    )
    loads = [pltpu.make_async_copy(src, dst, local_sem.at[i]) for i, (src, dst) in enumerate(pairs)]
    for load in loads[:2]:
        load.start()

    barrier = pltpu.get_barrier_semaphore()

    def greet(step, _):
        pl.semaphore_signal(barrier, inc=1, device_id=(lax.rem(me + step, n), block), device_id_type=MESH)
        return 0

    @pl.when(block > 0)
    def _():
        pl.semaphore_signal(barrier, inc=1, device_id=(me, block - 1), device_id_type=MESH)

    @pl.when(block < slabs - 1)
    def _():
        pl.semaphore_signal(barrier, inc=1, device_id=(me, block + 1), device_id_type=MESH)

    lax.fori_loop(1, n, greet, 0)

    def everyone_is_here():
        pl.semaphore_wait(barrier, n - 1 + (block > 0).astype(jnp.int32) + (block < slabs - 1).astype(jnp.int32))

    def to_block_before():
        return pltpu.make_async_remote_copy(
            src_ref=sigma.at[0, 0], dst_ref=sigma_v.at[1], send_sem=slab_send, recv_sem=slab_recv,
            device_id=(me, lax.max(block - 1, 0)), device_id_type=MESH,
        )

    term[...] = jnp.zeros_like(term)
    inner_v[...] = jnp.zeros_like(inner_v)
    loads[0].wait()
    loads[1].wait()
    for load in loads[2:]:
        load.start()

    @pl.when(block > 0)
    def _():
        everyone_is_here()
        to_block_before().start()

    def add_term(index, _):
        @pl.when(index == 1)
        def _():
            loads[2].wait()
            to_block_before().wait_recv()

        inner_v[:, :orbitals] = sigma_v[index, 0]
        inner_v[:, 2 * LANES:2 * LANES + orbitals] = sigma_v[index, 1]
        for group, value in enumerate(sandwich(outer_v.at[index], inner_v)):
            term[:orbitals, group * LANES:(group + 1) * LANES] += value
        return 0

    lax.fori_loop(0, 1 + (block < slabs - 1).astype(jnp.int32), add_term, 0)

    @pl.when(block == slabs - 1)
    def _():
        loads[2].wait()

    @pl.when(block == 0)
    def _():
        everyone_is_here()

    for owner in range(n):
        send1[owner * pitch:(owner + 1) * pitch] = term[owner * rows:owner * rows + pitch].astype(jnp.bfloat16)

    def at(ref, index):
        return ref.at[pl.ds(pl.multiple_of(index * pitch, pitch), pitch)]

    def copy(src, dst, send_sem, recv_sem, peer, slot):
        return pltpu.make_async_remote_copy(
            src_ref=at(src, peer), dst_ref=at(dst, slot), send_sem=send_sem.at[peer], recv_sem=recv_sem.at[slot],
            device_id=(peer, block), device_id_type=MESH,
        )

    def distance(turn):
        return turn + 1

    def each(act):
        def body(turn, _):
            act(distance(turn))
            return 0

        lax.fori_loop(0, n - 1, body, 0, unroll=n <= 16)

    first = (send1, recv1, send1_sem, recv1_sem)
    second = (send2, recv2, send2_sem, recv2_sem)

    def behind(step):
        return lax.rem(me + n - step, n)

    def ahead(step):
        return lax.rem(me + step, n)

    each(lambda step: copy(*first, ahead(step), me).start())
    own = pltpu.make_async_copy(at(send1, me), at(recv1, me), recv1_sem.at[me])
    own.start()

    loads[3].wait()
    for row in range(rows):
        where = pl.ds(row * length, length)
        for part in range(2):
            line = screened_v[part, :, row * orbitals:(row + 1) * orbitals].astype(jnp.float32)
            last = line[:, LANES:]
            lines[where, part * LANES:(part + 1) * LANES] = line[:, :LANES].astype(jnp.bfloat16)
            lines[where, (part + 2) * LANES:(part + 3) * LANES] = jnp.concatenate([last, last], axis=1).astype(jnp.bfloat16)
    loads[4].wait()
    waves = mul(inverse_v[...], lines[...])
    cosine = waves[:lag_rows] + waves[2 * lag_rows:3 * lag_rows]
    sine = waves[lag_rows:2 * lag_rows] + waves[3 * lag_rows:]
    for group in range(0, 4, 2):
        real, imag = (slice(part * LANES, (part + 1) * LANES) for part in (group, group + 1))
        for lag in range(n):
            here = slice(lag * pitch, (lag + 1) * pitch)
            lags[n - 1 + lag, :, real] = cosine[here, real] - sine[here, imag]
            lags[n - 1 + lag, :, imag] = cosine[here, imag] + sine[here, real]
            if lag > 0:
                lags[n - 1 - lag, :, real] = cosine[here, real] + sine[here, imag]
                lags[n - 1 - lag, :, imag] = cosine[here, imag] - sine[here, real]

    sign = jnp.where(lax.broadcasted_iota(jnp.int32, (pitch, LANES), 1) < tail, -1.0, 1.0)
    parts = tuple(slice(part * LANES, (part + 1) * LANES) for part in range(4))

    def take(source, buffer):
        rows_of = buffer[pl.ds(pl.multiple_of(source * pitch, pitch), pitch), :].astype(jnp.float32)
        real, imag, mixed = rows_of[:, parts[0]], rows_of[:, parts[1]], rows_of[:, parts[2]]
        return source, real, imag, mixed, pltpu.roll(mixed, tail, 1) * sign

    def terms(taken, energy):
        source, real, imag, mixed, turned = taken
        lag = energy - source + n - 1
        by_real, by_imag, both_real, both_imag = (lags[lag, :, part] for part in parts)
        return real * by_real - imag * by_imag, real * by_imag + imag * by_real, mixed * both_real + turned * both_imag

    own.wait()

    def both(turn):
        taken = []
        for source in (behind(distance(turn)), behind(distance(turn + 1))):
            copy(*first, source, source).wait_recv()
            taken.append(take(source, recv1))
        return taken

    def add(taken, energy):
        return [one + other for one, other in zip(terms(taken[0], energy), terms(taken[1], energy))]

    mine = take(me, recv1)
    source = behind(distance(0))
    copy(*first, source, source).wait_recv()
    taken = [mine, take(source, recv1)]

    def begin(energy, _):
        for part, value in zip(parts, add(taken, energy)):
            total[energy, :, part] = value
        return 0

    lax.fori_loop(0, n, begin, 0, unroll=n <= 16)

    def arrived(pair, _):
        taken = both(2 * pair + 1)
        for energy in range(n):
            for part, value in zip(parts, add(taken, energy)):
                total[energy, :, part] += value
        return 0

    lax.fori_loop(0, n // 2 - 2, arrived, 0)
    taken = both(n - 3)

    def finish(energy):
        where = pl.ds(pl.multiple_of(energy * pitch, pitch), pitch)
        for part, value in zip(parts, add(taken, energy)):
            send2[where, part] = (total[energy, :, part] + value).astype(jnp.bfloat16)

    def depart(step):
        finish(ahead(step))
        copy(*second, ahead(step), me).start()

    each(depart)
    finish(me)
    keep = pltpu.make_async_copy(at(send2, me), at(recv2, me), recv2_sem.at[me])
    keep.start()
    each(lambda step: copy(*first, ahead(step), me).wait_send())

    @pl.when(block > 0)
    def _():
        to_block_before().wait_send()

    each(lambda step: copy(*second, behind(step), behind(step)).wait_recv())
    keep.wait()
    each(lambda step: copy(*second, ahead(step), me).wait_send())


def unpack(rows, pitch, packed, out, spread):
    orbitals = out.shape[-1]
    tail = orbitals - LANES
    for owner in range(orbitals // rows):
        block = packed[owner * pitch:(owner + 1) * pitch].astype(jnp.float32)
        spread[owner * rows:owner * rows + pitch] = block
    result = spread[:orbitals].astype(jnp.bfloat16)
    out[0, 0, 0, :, :LANES] = result[:, :LANES]
    out[0, 0, 1, :, :LANES] = result[:, LANES:2 * LANES]
    out[0, 0, 0, :, LANES:] = result[:, 2 * LANES:2 * LANES + tail]
    out[0, 0, 1, :, LANES:] = result[:, 2 * LANES + tail:]


def shards(n, slabs, green_block, coupling, sigma_lesser, screened):
    orbitals = green_block.shape[-1]
    length = screened.shape[2]
    rows = screened.shape[3] // orbitals
    pitch = -(-rows // PITCH) * PITCH
    assert green_block.shape[0] == 1 and length == 2 * n and rows * n == orbitals and orbitals == LANES + LANES // 2
    inverse = make_tables(n, rows, pitch)
    packed = (n * pitch, 2 * orbitals)
    square = (2, orbitals, orbitals)
    bf16 = jnp.bfloat16
    returned = pl.pallas_call(
        functools.partial(kernel, n, slabs, rows, pitch),
        out_shape=pltpu.VMEM(packed, bf16),
        in_specs=[pl.BlockSpec(memory_space=pl.ANY)] * 5,
        out_specs=pl.BlockSpec(memory_space=pltpu.VMEM),
        scratch_shapes=[
            pltpu.VMEM((2, *square), bf16),
            pltpu.VMEM((2, *square), bf16),
            pltpu.VMEM((orbitals, 4 * LANES), bf16),
            pltpu.VMEM(screened.shape[1:], bf16),
            pltpu.VMEM(inverse.shape, bf16),
            pltpu.VMEM((rows * length, 4 * LANES), bf16),
            pltpu.VMEM((2 * n - 1, pitch, 4 * LANES), jnp.float32),
            pltpu.VMEM((n, pitch, 3 * LANES), jnp.float32),
            pltpu.VMEM((orbitals + pitch, 3 * LANES), jnp.float32),
            pltpu.VMEM(packed, bf16),
            pltpu.VMEM(packed, bf16),
            pltpu.VMEM(packed, bf16),
            pltpu.SemaphoreType.DMA((5,)),
            pltpu.SemaphoreType.DMA,
            pltpu.SemaphoreType.DMA,
            *[pltpu.SemaphoreType.DMA((n,))] * 4,
        ],
        compiler_params=pltpu.CompilerParams(
            collective_id=0, has_side_effects=True, vmem_limit_bytes=56 * 1024 * 1024
        ),
        cost_estimate=pl.CostEstimate(flops=10**9, bytes_accessed=4 * 10**6, transcendentals=0),
        name="self_energy",
    )(green_block, coupling, sigma_lesser, screened, jnp.asarray(inverse))
    return pl.pallas_call(
        functools.partial(unpack, rows, pitch),
        out_shape=jax.ShapeDtypeStruct(green_block.shape, bf16),
        in_specs=[pl.BlockSpec(memory_space=pltpu.VMEM)],
        out_specs=pl.BlockSpec(memory_space=pltpu.VMEM),
        scratch_shapes=[pltpu.VMEM((orbitals + pitch, 3 * LANES), jnp.float32)],
        name="unpack",
    )(pltpu.with_memory_space_constraint(returned, pltpu.VMEM))


def solution(mesh):
    placed = (
        P("energy", "slab", None, None, None),
        P("energy", "slab", None, None, None),
        P("energy", "slab", None, None, None),
        P("slab", None, None, "energy"),
    )
    return jax.shard_map(
        functools.partial(shards, mesh.shape["energy"], mesh.shape["slab"]),
        mesh=mesh,
        in_specs=placed,
        out_specs=P("energy", "slab", None, None, None),
        check_vma=False,
    )
```

```python
import functools

import jax
import jax.numpy as jnp
import ml_dtypes
import numpy as np
from jax import lax
from jax.experimental import pallas as pl
from jax.experimental.pallas import tpu as pltpu
from jax.sharding import PartitionSpec as P

MESH = pl.DeviceIdType.MESH
LANES = 128
PITCH = 16


def make_tables(count, rows, pitch):
    length = 2 * count
    phases = np.outer(np.arange(count), np.arange(length)) % length
    angles = phases * (2.0 * np.pi / length)
    same = np.zeros((pitch, rows))
    same[np.arange(rows), np.arange(rows)] = 1.0
    tables = []
    for table in (np.cos(angles), np.sin(angles)):
        wide = np.einsum("dk,sr->dsrk", table / length, same).reshape(count * pitch, rows * length)
        tables.append(wide.astype(ml_dtypes.bfloat16))
    return np.concatenate(tables, axis=0)


def mul(first, second):
    return jnp.dot(first, second, preferred_element_type=jnp.float32)


def mul_t(first, second):
    return lax.dot_general(first, second, (((1,), (1,)), ((), ())), preferred_element_type=jnp.float32)


def sandwich(outer, inner):
    orbitals = outer.shape[1]
    stacked = outer[...].reshape(2 * orbitals, orbitals)
    both = mul(stacked, inner[...])
    by_real, by_imag = both[:, :orbitals], both[:, 2 * LANES:2 * LANES + orbitals]
    half_real = by_real[:orbitals] - by_imag[orbitals:]
    half_imag = by_imag[:orbitals] + by_real[orbitals:]
    half = jnp.concatenate([half_real.astype(jnp.bfloat16), half_imag.astype(jnp.bfloat16)], axis=0)
    right = jnp.concatenate([outer[0], outer[0, LANES:], outer[1], outer[1, LANES:]], axis=0)
    both = mul_t(half, right)
    with_real, with_imag = both[:, :2 * LANES], both[:, 2 * LANES:]
    full_real = with_real[:orbitals] + with_imag[orbitals:]
    full_imag = with_real[orbitals:] - with_imag[:orbitals]
    low = lax.broadcasted_iota(jnp.int32, (orbitals, LANES), 1) < orbitals - LANES
    return full_real[:, :LANES], full_imag[:, :LANES], jnp.where(low, full_real[:, LANES:], full_imag[:, LANES:])


def kernel(
    n, slabs, rows, pitch,
    green, couple, sigma, screened, inverse,
    recv2,
    outer_v, sigma_v, inner_v, screened_v, inverse_v,
    lines, lags, total, term, send1, recv1, send2,
    local_sem, slab_send, slab_recv, send1_sem, recv1_sem, send2_sem, recv2_sem,
):
    me = lax.axis_index("energy")
    block = lax.axis_index("slab")
    orbitals = outer_v.shape[2]
    length = screened_v.shape[1]
    lag_rows = n * pitch
    tail = orbitals - LANES

    pairs = (
        (green.at[0, 0], outer_v.at[0]), (sigma.at[0, 0], sigma_v.at[0]), (couple.at[0, 0], outer_v.at[1]),
        (screened.at[0], screened_v), (inverse, inverse_v),
    )
    loads = [pltpu.make_async_copy(src, dst, local_sem.at[i]) for i, (src, dst) in enumerate(pairs)]
    for load in loads[:2]:
        load.start()

    barrier = pltpu.get_barrier_semaphore()

    def greet(step, _):
        pl.semaphore_signal(barrier, inc=1, device_id=(lax.rem(me + step, n), block), device_id_type=MESH)
        return 0

    @pl.when(block > 0)
    def _():
        pl.semaphore_signal(barrier, inc=1, device_id=(me, block - 1), device_id_type=MESH)

    @pl.when(block < slabs - 1)
    def _():
        pl.semaphore_signal(barrier, inc=1, device_id=(me, block + 1), device_id_type=MESH)

    lax.fori_loop(1, n, greet, 0)

    def everyone_is_here():
        pl.semaphore_wait(barrier, n - 1 + (block > 0).astype(jnp.int32) + (block < slabs - 1).astype(jnp.int32))

    def to_block_before():
        return pltpu.make_async_remote_copy(
            src_ref=sigma.at[0, 0], dst_ref=sigma_v.at[1], send_sem=slab_send, recv_sem=slab_recv,
            device_id=(me, lax.max(block - 1, 0)), device_id_type=MESH,
        )

    term[...] = jnp.zeros_like(term)
    inner_v[...] = jnp.zeros_like(inner_v)
    loads[0].wait()
    loads[1].wait()
    for load in loads[2:]:
        load.start()

    @pl.when(block > 0)
    def _():
        everyone_is_here()
        to_block_before().start()

    def add_term(index, _):
        @pl.when(index == 1)
        def _():
            loads[2].wait()
            to_block_before().wait_recv()

        inner_v[:, :orbitals] = sigma_v[index, 0]
        inner_v[:, 2 * LANES:2 * LANES + orbitals] = sigma_v[index, 1]
        for group, value in enumerate(sandwich(outer_v.at[index], inner_v)):
            term[:orbitals, group * LANES:(group + 1) * LANES] += value
        return 0

    lax.fori_loop(0, 1 + (block < slabs - 1).astype(jnp.int32), add_term, 0)

    @pl.when(block == slabs - 1)
    def _():
        loads[2].wait()

    @pl.when(block == 0)
    def _():
        everyone_is_here()

    for owner in range(n):
        send1[owner * pitch:(owner + 1) * pitch] = term[owner * rows:owner * rows + pitch].astype(jnp.bfloat16)

    def at(ref, index):
        return ref.at[pl.ds(pl.multiple_of(index * pitch, pitch), pitch)]

    def copy(src, dst, send_sem, recv_sem, peer, slot):
        return pltpu.make_async_remote_copy(
            src_ref=at(src, peer), dst_ref=at(dst, slot), send_sem=send_sem.at[peer], recv_sem=recv_sem.at[slot],
            device_id=(peer, block), device_id_type=MESH,
        )

    def distance(turn):
        return turn + 1

    def each(act):
        def body(turn, _):
            act(distance(turn))
            return 0

        lax.fori_loop(0, n - 1, body, 0, unroll=n <= 16)

    first = (send1, recv1, send1_sem, recv1_sem)
    second = (send2, recv2, send2_sem, recv2_sem)

    def behind(step):
        return lax.rem(me + n - step, n)

    def ahead(step):
        return lax.rem(me + step, n)

    each(lambda step: copy(*first, ahead(step), me).start())
    own = pltpu.make_async_copy(at(send1, me), at(recv1, me), recv1_sem.at[me])
    own.start()

    loads[3].wait()
    for row in range(rows):
        where = pl.ds(row * length, length)
        for part in range(2):
            line = screened_v[part, :, row * orbitals:(row + 1) * orbitals].astype(jnp.float32)
            last = line[:, LANES:]
            lines[where, part * LANES:(part + 1) * LANES] = line[:, :LANES].astype(jnp.bfloat16)
            lines[where, (part + 2) * LANES:(part + 3) * LANES] = jnp.concatenate([last, last], axis=1).astype(jnp.bfloat16)
    loads[4].wait()
    waves = mul(inverse_v[...], lines[...])
    cosine, sine = waves[:lag_rows], waves[lag_rows:]
    for group in range(0, 4, 2):
        real, imag = (slice(part * LANES, (part + 1) * LANES) for part in (group, group + 1))
        for lag in range(n):
            here = slice(lag * pitch, (lag + 1) * pitch)
            lags[n - 1 + lag, :, real] = cosine[here, real] - sine[here, imag]
            lags[n - 1 + lag, :, imag] = cosine[here, imag] + sine[here, real]
            if lag > 0:
                lags[n - 1 - lag, :, real] = cosine[here, real] + sine[here, imag]
                lags[n - 1 - lag, :, imag] = cosine[here, imag] - sine[here, real]

    sign = jnp.where(lax.broadcasted_iota(jnp.int32, (pitch, LANES), 1) < tail, -1.0, 1.0)
    parts = tuple(slice(part * LANES, (part + 1) * LANES) for part in range(4))

    def take(source, buffer):
        rows_of = buffer[pl.ds(pl.multiple_of(source * pitch, pitch), pitch), :].astype(jnp.float32)
        real, imag, mixed = rows_of[:, parts[0]], rows_of[:, parts[1]], rows_of[:, parts[2]]
        return source, real, imag, mixed, pltpu.roll(mixed, tail, 1) * sign

    def terms(taken, energy):
        source, real, imag, mixed, turned = taken
        lag = energy - source + n - 1
        by_real, by_imag, both_real, both_imag = (lags[lag, :, part] for part in parts)
        return real * by_real - imag * by_imag, real * by_imag + imag * by_real, mixed * both_real + turned * both_imag

    own.wait()

    def both(turn):
        taken = []
        for source in (behind(distance(turn)), behind(distance(turn + 1))):
            copy(*first, source, source).wait_recv()
            taken.append(take(source, recv1))
        return taken

    def add(taken, energy):
        return [one + other for one, other in zip(terms(taken[0], energy), terms(taken[1], energy))]

    mine = take(me, recv1)
    source = behind(distance(0))
    copy(*first, source, source).wait_recv()
    taken = [mine, take(source, recv1)]

    def begin(energy, _):
        for part, value in zip(parts, add(taken, energy)):
            total[energy, :, part] = value
        return 0

    lax.fori_loop(0, n, begin, 0, unroll=n <= 16)

    def arrived(pair, _):
        taken = both(2 * pair + 1)
        for energy in range(n):
            for part, value in zip(parts, add(taken, energy)):
                total[energy, :, part] += value
        return 0

    lax.fori_loop(0, n // 2 - 2, arrived, 0)
    taken = both(n - 3)

    def finish(energy):
        where = pl.ds(pl.multiple_of(energy * pitch, pitch), pitch)
        for part, value in zip(parts, add(taken, energy)):
            send2[where, part] = (total[energy, :, part] + value).astype(jnp.bfloat16)

    def depart(step):
        finish(ahead(step))
        copy(*second, ahead(step), me).start()

    each(depart)
    finish(me)
    keep = pltpu.make_async_copy(at(send2, me), at(recv2, me), recv2_sem.at[me])
    keep.start()
    each(lambda step: copy(*first, ahead(step), me).wait_send())

    @pl.when(block > 0)
    def _():
        to_block_before().wait_send()

    each(lambda step: copy(*second, behind(step), behind(step)).wait_recv())
    keep.wait()
    each(lambda step: copy(*second, ahead(step), me).wait_send())


def unpack(rows, pitch, packed, out, spread):
    orbitals = out.shape[-1]
    tail = orbitals - LANES
    for owner in range(orbitals // rows):
        block = packed[owner * pitch:(owner + 1) * pitch].astype(jnp.float32)
        spread[owner * rows:owner * rows + pitch] = block
    result = spread[:orbitals].astype(jnp.bfloat16)
    out[0, 0, 0, :, :LANES] = result[:, :LANES]
    out[0, 0, 1, :, :LANES] = result[:, LANES:2 * LANES]
    out[0, 0, 0, :, LANES:] = result[:, 2 * LANES:2 * LANES + tail]
    out[0, 0, 1, :, LANES:] = result[:, 2 * LANES + tail:]


def shards(n, slabs, green_block, coupling, sigma_lesser, screened):
    orbitals = green_block.shape[-1]
    length = screened.shape[2]
    rows = screened.shape[3] // orbitals
    pitch = -(-rows // PITCH) * PITCH
    assert green_block.shape[0] == 1 and length == 2 * n and rows * n == orbitals and orbitals == LANES + LANES // 2
    inverse = make_tables(n, rows, pitch)
    packed = (n * pitch, 2 * orbitals)
    square = (2, orbitals, orbitals)
    bf16 = jnp.bfloat16
    returned = pl.pallas_call(
        functools.partial(kernel, n, slabs, rows, pitch),
        out_shape=pltpu.VMEM(packed, bf16),
        in_specs=[pl.BlockSpec(memory_space=pl.ANY)] * 5,
        out_specs=pl.BlockSpec(memory_space=pltpu.VMEM),
        scratch_shapes=[
            pltpu.VMEM((2, *square), bf16),
            pltpu.VMEM((2, *square), bf16),
            pltpu.VMEM((orbitals, 4 * LANES), bf16),
            pltpu.VMEM(screened.shape[1:], bf16),
            pltpu.VMEM(inverse.shape, bf16),
            pltpu.VMEM((rows * length, 4 * LANES), bf16),
            pltpu.VMEM((2 * n - 1, pitch, 4 * LANES), jnp.float32),
            pltpu.VMEM((n, pitch, 3 * LANES), jnp.float32),
            pltpu.VMEM((orbitals + pitch, 3 * LANES), jnp.float32),
            pltpu.VMEM(packed, bf16),
            pltpu.VMEM(packed, bf16),
            pltpu.VMEM(packed, bf16),
            pltpu.SemaphoreType.DMA((5,)),
            pltpu.SemaphoreType.DMA,
            pltpu.SemaphoreType.DMA,
            *[pltpu.SemaphoreType.DMA((n,))] * 4,
        ],
        compiler_params=pltpu.CompilerParams(
            collective_id=0, has_side_effects=True, vmem_limit_bytes=56 * 1024 * 1024
        ),
        cost_estimate=pl.CostEstimate(flops=10**9, bytes_accessed=4 * 10**6, transcendentals=0),
        name="self_energy",
    )(green_block, coupling, sigma_lesser, screened, jnp.asarray(inverse))
    return pl.pallas_call(
        functools.partial(unpack, rows, pitch),
        out_shape=jax.ShapeDtypeStruct(green_block.shape, bf16),
        in_specs=[pl.BlockSpec(memory_space=pltpu.VMEM)],
        out_specs=pl.BlockSpec(memory_space=pltpu.VMEM),
        scratch_shapes=[pltpu.VMEM((orbitals + pitch, 3 * LANES), jnp.float32)],
        name="unpack",
    )(pltpu.with_memory_space_constraint(returned, pltpu.VMEM))


def solution(mesh):
    placed = (
        P("energy", "slab", None, None, None),
        P("energy", "slab", None, None, None),
        P("energy", "slab", None, None, None),
        P("slab", None, None, "energy"),
    )
    return jax.shard_map(
        functools.partial(shards, mesh.shape["energy"], mesh.shape["slab"]),
        mesh=mesh,
        in_specs=placed,
        out_specs=P("energy", "slab", None, None, None),
        check_vma=False,
    )
```
